128 devices in a mesh: rep: 2 (over y_lo), section: 8 (over y_hi, z), tp: 8 (over x, core).
Axes of the slice: x: 4, y: 4 (y_hi: 2, y_lo: 2; y = y_hi * 2 + y_lo), z: 4, core: 2. Of those that a mesh axis runs over, the one named last changes fastest.
Arguments:
- hidden: bfloat16 [2, 8, 16, 8192], P('rep', 'section'), may hold values from -6 to 6
- gain: float32 [8, 8192], P('section'), may hold values from 0.25 to 1.75
- w_query: bfloat16 [8, 8192, 4096], P('section', None, 'tp'), may hold values from -0.0625 to 0.0625
- w_keyval: bfloat16 [2, 8, 8192, 2048], P('rep', 'section', None, 'tp'), may hold values from -0.0625 to 0.0625
- w_out: bfloat16 [8, 4096, 8192], P('section', 'tp'), may hold values from -0.09375 to 0.09375
- old_pool: bfloat16 [4096, 32, 2048], P(('rep', 'section'), None, 'tp'), may hold values from -6 to 6
- send_index: int32 [16, 16, 32], P(('rep', 'section')), may hold values from 0 to 255
- recv_slot: int32 [16, 16, 32], P(('rep', 'section')), may hold values from 0 to 256, as said below
- holder: int32 [8], P('section'), may hold values from 0 to 1
- lengths: int32 [2, 8, 16], P('rep', 'section'), may hold values from 1 to 511, as said below
Outputs:
- next_hidden: bfloat16 [2, 8, 16, 8192], P('rep', 'section')
- cache: bfloat16 [2, 8, 16, 512, 2048], P('rep', 'section', None, None, 'tp')
The draws below stay inside these ranges and needn't reach their ends.
Inputs may be any that keep to these rules, and one draw needn't show every extreme that they name: For every owner, each of its 256 block numbers appears exactly once in recv_slot[owner]; the other entries are 256. In every owner's row one holder fills all 32 slots. `lengths`: on every section of every replica one request has 511 positions.
All inputs are finite; a program needn't handle non-finite values.
Results may differ from the reference program's by a relative error of at most 0.004.
Values may be sent and summed in bfloat16 or wider, within the bound.
A program may use at most 128 MiB of HBM per device.

```python
import jax
import jax.numpy as jnp
from jax import lax

D = 8192
QH = 32
KVH = 8
HD = 128
REQ_DEV = 16
CTX = 512
BLK = 32
NB_DEV = 256
CAP = 32
POOL = 256
N_REP = 2
N_SECTION = 8


def draw_recv_slot(key, part):
    key = jax.random.fold_in(key, 11)
    groups = N_REP * N_SECTION
    tickets = groups * CAP
    keys = jax.random.split(key, groups)

    def one_owner(owner_key):
        first, second, third = jax.random.split(owner_key, 3)
        filler = jax.random.randint(first, (), 0, groups, dtype=jnp.int32)
        rank = jax.random.permutation(second, tickets).astype(jnp.int32)
        source = jnp.arange(tickets, dtype=jnp.int32) // CAP
        score = jnp.where(source == filler, 0, 1 + rank)
        order = jnp.argsort(score, stable=True)
        slots = jax.random.permutation(third, NB_DEV).astype(jnp.int32)
        table = jnp.full((tickets,), NB_DEV, jnp.int32).at[order[:NB_DEV]].set(slots)
        return table.reshape(groups, CAP)
    return jax.vmap(one_owner)(keys).astype(jnp.int32)


def draw_lengths(key, part):
    key = jax.random.fold_in(key, 12)
    first, second = jax.random.split(key)
    base = jax.random.randint(first, (N_REP, N_SECTION, REQ_DEV), 1, CTX, dtype=jnp.int32)
    where_full = jax.random.randint(second, (N_REP, N_SECTION, 1), 0, REQ_DEV, dtype=jnp.int32)
    column = jnp.arange(REQ_DEV, dtype=jnp.int32)[None, None, :]
    return jnp.where(column == where_full, CTX - 1, base).astype(jnp.int32)


def plant(entries, rng, smallest, top_value):
    index_at = [jax.random.randint(jax.random.fold_in(rng, axis), (), 0, length) for axis, length in enumerate(entries.shape)]
    main_axis = entries.shape.index(max(entries.shape))
    beside = index_at[:main_axis] + [(index_at[main_axis] + 1) % entries.shape[main_axis]] + index_at[main_axis + 1:]
    return entries.at[tuple(index_at)].set(smallest).at[tuple(beside)].set(top_value)


def levels(stream_key, shape, cuts, least, largest):
    def one(dim, parts):
        draws = jax.random.uniform(jax.random.fold_in(jax.random.fold_in(stream_key, 6), dim), (parts,), jnp.float32, least / len(cuts), largest / len(cuts))
        return jnp.repeat(jnp.exp(draws), shape[dim] // parts).reshape((-1,) + (1,) * (len(shape) - dim - 1))

    loudness = one(*cuts[0])
    for cut in cuts[1:]:
        loudness = loudness * one(*cut)
    return loudness


def scatter_about(rng, extent, spread, bound, pieces=(), held_as=jnp.bfloat16):
    level = levels(rng, extent, pieces, -0.22, 0.18) if pieces else 1.0
    result = jax.random.normal(rng, extent, jnp.float32) * spread * level
    return jnp.minimum(jnp.maximum(result, -bound), bound).astype(held_as)


def setup_inputs(seed: int = 0) -> dict:
    seeds = jax.random.split(jax.random.key(seed), 11)
    hidden = scatter_about(seeds[0], (N_REP, N_SECTION, REQ_DEV, D), 1.0, 6.0, ((0, 2), (1, 8)))
    gain = jnp.clip(1.0 + 0.15 * jax.random.normal(seeds[1], (N_SECTION, D), jnp.float32), 0.25, 1.75)
    w_query = scatter_about(seeds[2], (N_SECTION, D, QH * HD), D ** -0.5, 0.0625, ((0, 8), (2, 8)))
    w_keyval = scatter_about(seeds[3], (N_REP, N_SECTION, D, KVH * 2 * HD), D ** -0.5, 0.0625, ((0, 2), (1, 8), (3, 8)))
    w_out = scatter_about(seeds[4], (N_SECTION, QH * HD, D), (QH * HD) ** -0.5, 0.09375, ((0, 8), (1, 8)))
    old_pool = scatter_about(seeds[5], (N_REP * N_SECTION * POOL, BLK, KVH * 2 * HD), 1.0, 6.0, ((0, 16), (2, 8)))
    send_index = plant(jax.random.randint(seeds[6], (N_REP * N_SECTION, N_REP * N_SECTION, CAP), 0, POOL), jax.random.fold_in(seeds[6], 1), 0, POOL - 1).astype(jnp.int32)
    recv_slot = draw_recv_slot(jax.random.fold_in(seeds[10], 71), 0)
    holder = plant(jax.random.randint(seeds[8], (N_SECTION,), 0, N_REP), jax.random.fold_in(seeds[8], 1), 0, N_REP - 1).astype(jnp.int32)
    lengths = draw_lengths(jax.random.fold_in(seeds[10], 71), 0)
    return dict(hidden=hidden, gain=gain, w_query=w_query, w_keyval=w_keyval, w_out=w_out, old_pool=old_pool, send_index=send_index, recv_slot=recv_slot, holder=holder, lengths=lengths)


def reference(hidden, gain, w_query, w_keyval, w_out, old_pool, send_index, recv_slot, holder, lengths):
    groups = N_REP * N_SECTION
    width = KVH * 2 * HD
    nblock = REQ_DEV * (CTX // BLK)
    group_size = QH // KVH
    positions = jnp.arange(CTX, dtype=jnp.int32)
    results = []
    caches = []
    for owner in range(groups):
        rep_idx = owner // N_SECTION
        section_idx = owner % N_SECTION
        rows = (jnp.arange(groups, dtype=jnp.int32)[:, None] * POOL + send_index[:, owner, :]).reshape(-1)
        blocks = old_pool[rows]
        slots = recv_slot[owner].reshape(-1)
        moved = jnp.zeros((nblock, BLK, width), jnp.bfloat16).at[slots].set(blocks, mode='drop')
        moved = moved.reshape(REQ_DEV, CTX, width)
        state = hidden[rep_idx, section_idx].astype(jnp.float32)
        scale = jax.lax.rsqrt(lax.optimization_barrier(jnp.mean(state * state, axis=-1, keepdims=True)) + 1e-05)
        normed = (state * scale * gain[section_idx]).astype(jnp.bfloat16)
        query = jnp.dot(normed, w_query[section_idx], preferred_element_type=jnp.float32).astype(jnp.bfloat16)
        keyval = jnp.dot(normed, w_keyval[holder[section_idx], section_idx], preferred_element_type=jnp.float32).astype(jnp.bfloat16)
        length = lengths[rep_idx, section_idx]
        cache = jnp.where(positions[None, :, None] == length[:, None, None], keyval[:, None, :], moved)
        caches.append(cache)
        split = cache.reshape(REQ_DEV, CTX, KVH, 2, HD)
        keys = split[:, :, :, 0, :].astype(jnp.float32)
        values = split[:, :, :, 1, :].astype(jnp.float32)
        heads = query.reshape(REQ_DEV, KVH, group_size, HD).astype(jnp.float32)
        scores = jnp.einsum('bhgd,bjhd->bhgj', heads, keys) * HD ** (-0.5)
        valid = positions[None, None, None, :] <= length[:, None, None, None]
        expo = jnp.where(valid, jnp.exp(jnp.where(valid, scores, 0.0)), 0.0)
        probs = expo / lax.optimization_barrier(jnp.sum(expo, axis=-1, keepdims=True))
        weights = probs.astype(jnp.bfloat16).astype(jnp.float32)
        attended = jnp.einsum('bhgj,bjhd->bhgd', weights, values).astype(jnp.bfloat16).reshape(REQ_DEV, QH * HD)
        update = jnp.dot(attended, w_out[section_idx], preferred_element_type=jnp.float32)
        results.append((state + update).astype(jnp.bfloat16))
    after = jnp.stack(results).reshape(N_REP, N_SECTION, REQ_DEV, D)
    cache_all = jnp.stack(caches).reshape(N_REP, N_SECTION, REQ_DEV, CTX, width)
    return (jnp.roll(after, 1, axis=1), cache_all)
```

```python
import functools

import jax
import jax.numpy as jnp
from jax import lax
from jax.experimental import pallas as pl
from jax.experimental.pallas import tpu as pltpu
from jax.sharding import PartitionSpec as P

HD = 128
CTX = 512
BLK = 32
MESH = pl.DeviceIdType.MESH
MIB = 2**20
FAR = (1, 3, 2)


def place():
    rep, section = lax.axis_index("rep"), lax.axis_index("section")
    return (section // 4) * 2 + rep, section % 4, lax.axis_index("tp")


def at(y, z):
    return {"rep": y % 2, "section": (y // 2) * 4 + z}


def group(y, z):
    return (y % 2) * 8 + (y // 2) * 4 + z


def remote(src, dst, send, recv, k, device):
    return pltpu.make_async_remote_copy(
        src_ref=src,
        dst_ref=dst,
        send_sem=send.at[k],
        recv_sem=recv.at[k],
        device_id=device,
        device_id_type=MESH,
    )


def move_kernel(
    sidx, holder, hidden, gain, pool_h, wq_h, wkv_h,
    land, q_o, kv_o,
    pool, stage, mid_a, mid_b, wq, wkv, hpeer, kvsend, kvpeer, normed,
    send, recv, side_send, side_recv, local,
):
    y, z, _ = place()
    rep = lax.axis_index("rep")
    half = stage.shape[1] // 2
    lo, hi = pl.ds(0, half), pl.ds(half, half)

    pool_in = pltpu.make_async_copy(pool_h, pool, local.at[0])
    pool_in.start()
    wkv_in = pltpu.make_async_copy(wkv_h, wkv, local.at[1])
    wq_in = pltpu.make_async_copy(wq_h, wq, local.at[2])

    barrier = pltpu.get_barrier_semaphore()
    for d in FAR:
        for device in (at((y + d) % 4, z), at(y, (z + d) % 4)):
            pl.semaphore_signal(barrier, inc=1, device_id=device, device_id_type=MESH)
    pl.semaphore_wait(barrier, 6)

    peer = {"rep": 1 - rep}
    to_peer = remote(hidden, hpeer, side_send, side_recv, 0, peer)
    to_peer.start()
    pool_in.wait()
    wkv_in.start()
    wq_in.start()

    def fill(dy, dz):
        g = group((y + dy) % 4, (z + dz) % 4)

        def body(i, _):
            for u in range(4):
                c = i * 4 + u
                stage[dy * 4 + dz, c] = pool[sidx[g, c]]
            return 0

        lax.fori_loop(0, stage.shape[1] // 4, body, 0)

    me = group(y, z)
    down, across = {}, {}
    for dz in FAR:
        for dy in FAR:
            fill(dy, dz)
            k = (dy - 1) * 3 + dz - 1
            src = stage.at[dy * 4 + dz]
            down[dy, dz] = remote(src.at[lo], mid_a.at[k], send, recv, k, at((y + dy) % 4, z))
            across[dy, dz] = remote(src.at[hi], mid_b.at[k], send, recv, 9 + k, at(y, (z + dz) % 4))
            down[dy, dz].start()
            across[dy, dz].start()
    last = []
    late = []
    for d in FAR:
        fill(d, 0)
        fill(0, d)
        along_y, along_z = stage.at[d * 4], stage.at[d]
        for first, src, part, k, device in (
            (True, along_y, lo, 18 + d - 1, at((y + d) % 4, z)),
            (True, along_z, hi, 21 + d - 1, at(y, (z + d) % 4)),
            (False, along_y, hi, 24 + d - 1, at((y + d) % 4, z)),
            (False, along_z, lo, 27 + d - 1, at(y, (z + d) % 4)),
        ):
            copy = remote(src.at[part], land.at[me, part], send, recv, k, device)
            (last if first else late).append(copy)
            if first:
                copy.start()
    fill(0, 0)
    keep = pltpu.make_async_copy(stage.at[0], land.at[me], local.at[3])
    keep.start()

    to_peer.wait_recv()
    width = hidden.shape[1]
    step = 1024
    rows = hidden.shape[0]

    def scale_of(ref):
        total = jnp.zeros((rows, 1), jnp.float32)
        for i in range(width // step):
            part = ref[:, i * step : (i + 1) * step].astype(jnp.float32)
            total = total + jnp.sum(part * part, axis=1, keepdims=True)
        return lax.rsqrt(total / width + 1e-05)

    own_scale, peer_scale = scale_of(hidden), scale_of(hpeer)
    for i in range(width // step):
        cut = slice(i * step, (i + 1) * step)
        g = gain[:, cut]
        normed[0:rows, cut] = (hidden[:, cut].astype(jnp.float32) * own_scale * g).astype(jnp.bfloat16)
        normed[rows : 2 * rows, cut] = (hpeer[:, cut].astype(jnp.float32) * peer_scale * g).astype(jnp.bfloat16)

    def product(count, weight):
        def body(i, total):
            cut = pl.ds(pl.multiple_of(i * step, step), step)
            return total + jnp.dot(normed[0:count, cut], weight[cut, :], preferred_element_type=jnp.float32)

        return lax.fori_loop(0, width // step, body, jnp.zeros((count, weight.shape[1]), jnp.float32))

    wkv_in.wait()
    both = product(2 * rows, wkv).astype(jnp.bfloat16)
    kvsend[...] = both[rows : 2 * rows]
    back = remote(kvsend, kvpeer, side_send, side_recv, 1, peer)
    back.start()
    wq_in.wait()
    query = product(rows, wq).astype(jnp.bfloat16).astype(jnp.float32)
    q_o[...] = jnp.zeros_like(q_o)
    for h in range(query.shape[1] // HD):
        q_o[:, h, :] = query[:, h * HD : (h + 1) * HD]

    for copy in late:
        copy.start()
    relays = []
    for dz in FAR:
        for dy in FAR:
            k = (dy - 1) * 3 + dz - 1
            down[dy, dz].wait_recv()
            source = group((y - dy + 4) % 4, z)
            relay = remote(mid_a.at[k], land.at[source, lo], send, recv, 30 + k, at(y, (z + dz) % 4))
            relay.start()
            relays.append(relay)
            across[dy, dz].wait_recv()
            source = group(y, (z - dz + 4) % 4)
            relay = remote(mid_b.at[k], land.at[source, hi], send, recv, 39 + k, at((y + dy) % 4, z))
            relay.start()
            relays.append(relay)

    back.wait_recv()
    mine = jnp.where(holder[0] == rep, jnp.float32(1), jnp.float32(0))
    own = both[0:rows].astype(jnp.float32)
    other = kvpeer[...].astype(jnp.float32)
    kv_o[...] = jnp.where(jnp.full(own.shape, mine) > 0.5, own, other).astype(jnp.bfloat16)

    for copy in last + late + relays:
        copy.wait_recv()
    for copy in [*down.values(), *across.values(), *last, *late, *relays, to_peer, back]:
        copy.wait_send()
    keep.wait()


def attend_kernel(inv, lengths, land, q, kv, w_h, cache, out, held, w, att, sems):
    w_in = pltpu.make_async_copy(w_h, w, sems.at[0])
    blocks = held.shape[0]

    def fetch(i, _):
        for u in range(8):
            j = i * 8 + u
            pltpu.make_async_copy(land.at[inv[j]], held.at[j], sems.at[1]).start()
        return 0

    lax.fori_loop(0, blocks // 8, fetch, 0)
    w_in.start()
    pltpu.make_async_copy(land.at[pl.ds(0, blocks)], held, sems.at[1]).wait()

    requests = q.shape[0]
    per = blocks // requests
    row = lax.broadcasted_iota(jnp.int32, held.shape[1:], 0)

    for b in range(requests):
        length = lengths[b]
        j = b * per + length // BLK
        held[j] = jnp.where(row == length % BLK, kv[b : b + 1, :].astype(jnp.float32), held[j].astype(jnp.float32)).astype(jnp.bfloat16)
    store = pltpu.make_async_copy(held, cache, sems.at[2])
    store.start()

    position = lax.broadcasted_iota(jnp.int32, (q.shape[1], CTX), 1)

    for b in range(requests):
        keys = held[b * per : (b + 1) * per, :, 0:HD].reshape(CTX, HD)
        values = held[b * per : (b + 1) * per, :, HD : 2 * HD].reshape(CTX, HD)
        scores = lax.dot_general(
            q[b].astype(jnp.bfloat16), keys, (((1,), (1,)), ((), ())), preferred_element_type=jnp.float32
        ) * HD ** (-0.5)
        valid = position <= lengths[b]
        expo = jnp.where(valid, jnp.exp(jnp.where(valid, scores, 0.0)), 0.0)
        weights = (expo / jnp.sum(expo, axis=1, keepdims=True)).astype(jnp.bfloat16)
        att[b] = jnp.dot(weights, values, preferred_element_type=jnp.float32)

    heads = w.shape[0] // HD
    attended = jnp.concatenate([att[:, h, :] for h in range(heads)], axis=1).astype(jnp.bfloat16)
    w_in.wait()
    step = 1024

    def body(i, _):
        cut = pl.ds(pl.multiple_of(i * step, step), step)
        out[:, cut] = jnp.dot(attended, w[:, cut], preferred_element_type=jnp.float32)
        return 0

    lax.fori_loop(0, w.shape[1] // step, body, 0)
    store.wait()


def sum_kernel(part, hidden, out, land, mine, send, recv):
    tp = lax.axis_index("tp")
    section = lax.axis_index("section")
    sections = lax.axis_size("section")
    count = lax.axis_size("tp")
    step = part.shape[1] // count

    def cut(t):
        return pl.ds(pl.multiple_of(t * step, step), step)

    barrier = pltpu.get_barrier_semaphore()
    for k in range(1, count):
        pl.semaphore_signal(barrier, inc=1, device_id={"tp": (tp + k) % count}, device_id_type=MESH)
    before = {"section": (section + sections - 1) % sections}
    pl.semaphore_signal(barrier, inc=1, device_id=before, device_id_type=MESH)
    pl.semaphore_wait(barrier, count)

    sums = []
    for k in range(1, count):
        t = (tp + k) % count
        copy = remote(part.at[:, cut(t)], land.at[k - 1], send, recv, k - 1, {"tp": t})
        copy.start()
        sums.append(copy)
    total = hidden[:, cut(tp)].astype(jnp.float32) + part[:, cut(tp)]
    for k in range(1, count):
        sums[k - 1].wait_recv()
        total = total + land[k - 1]
    mine[...] = total.astype(jnp.bfloat16)
    shift = remote(mine, out.at[:, cut(tp)], send, recv, count - 1, {"section": (section + 1) % sections})
    shift.start()
    shift.wait_recv()
    spread = []
    for k in range(1, count):
        copy = remote(out.at[:, cut(tp)], out.at[:, cut(tp)], send, recv, count + k - 1, {"tp": (tp + k) % count})
        copy.start()
        spread.append(copy)
    for copy in spread:
        copy.wait_recv()
    for copy in [*sums, shift, *spread]:
        copy.wait_send()


def shards(
    hidden, gain, w_query, w_keyval, w_out, old_pool, send_index, recv_slot, holder, lengths
):
    state = hidden[0, 0]
    requests, width = state.shape
    pool_blocks, blk, lanes = old_pool.shape
    groups, cap = send_index.shape[1:]
    blocks = requests * CTX // blk
    heads = w_query.shape[2] // HD
    vmem = pl.BlockSpec(memory_space=pltpu.VMEM)
    smem = pl.BlockSpec(memory_space=pltpu.SMEM)
    hbm = pl.BlockSpec(memory_space=pl.ANY)

    slots = recv_slot[0].reshape(1, -1)
    hit = slots == jnp.arange(blocks, dtype=jnp.int32)[:, None]
    inverse = jnp.sum(jnp.where(hit, jnp.arange(groups * cap, dtype=jnp.int32)[None, :], 0), axis=1)

    half = cap // 2
    land, query, keyval = pl.pallas_call(
        move_kernel,
        name="move",
        out_shape=(
            jax.ShapeDtypeStruct((groups, cap, blk, lanes), jnp.bfloat16),
            jax.ShapeDtypeStruct((requests, 8, HD), jnp.float32),
            jax.ShapeDtypeStruct((requests, lanes), jnp.bfloat16),
        ),
        in_specs=[smem, smem, vmem, vmem, hbm, hbm, hbm],
        out_specs=(hbm, vmem, vmem),
        scratch_shapes=[
            pltpu.VMEM((pool_blocks, blk, lanes), jnp.bfloat16),
            pltpu.VMEM((groups, cap, blk, lanes), jnp.bfloat16),
            pltpu.VMEM((9, half, blk, lanes), jnp.bfloat16),
            pltpu.VMEM((9, half, blk, lanes), jnp.bfloat16),
            pltpu.VMEM(w_query.shape[1:], jnp.bfloat16),
            pltpu.VMEM(w_keyval.shape[2:], jnp.bfloat16),
            pltpu.VMEM((requests, width), jnp.bfloat16),
            pltpu.VMEM((requests, lanes), jnp.bfloat16),
            pltpu.VMEM((requests, lanes), jnp.bfloat16),
            pltpu.VMEM((2 * requests, width), jnp.bfloat16),
            pltpu.SemaphoreType.DMA((48,)),
            pltpu.SemaphoreType.DMA((48,)),
            pltpu.SemaphoreType.DMA((2,)),
            pltpu.SemaphoreType.DMA((2,)),
            pltpu.SemaphoreType.DMA((4,)),
        ],
        compiler_params=pltpu.CompilerParams(
            collective_id=0, has_side_effects=True, vmem_limit_bytes=42 * MIB
        ),
    )(send_index[0], holder, state, gain, old_pool, w_query[0], w_keyval[0, 0])

    cache, part = pl.pallas_call(
        attend_kernel,
        name="attend",
        out_shape=(
            jax.ShapeDtypeStruct((blocks, blk, lanes), jnp.bfloat16),
            jax.ShapeDtypeStruct((requests, width), jnp.float32),
        ),
        in_specs=[smem, smem, hbm, vmem, vmem, hbm],
        out_specs=(hbm, vmem),
        scratch_shapes=[
            pltpu.VMEM((blocks, blk, lanes), jnp.bfloat16),
            pltpu.VMEM(w_out.shape[1:], jnp.bfloat16),
            pltpu.VMEM((requests, 8, HD), jnp.float32),
            pltpu.SemaphoreType.DMA((3,)),
        ],
        compiler_params=pltpu.CompilerParams(vmem_limit_bytes=24 * MIB),
    )(inverse, lengths[0, 0], land.reshape(groups * cap, blk, lanes), query, keyval, w_out[0])

    tp = lax.axis_size("tp")
    passed = pl.pallas_call(
        sum_kernel,
        name="sum",
        out_shape=jax.ShapeDtypeStruct((requests, width), jnp.bfloat16),
        in_specs=[vmem, vmem],
        out_specs=vmem,
        scratch_shapes=[
            pltpu.VMEM((tp - 1, requests, width // tp), jnp.float32),
            pltpu.VMEM((requests, width // tp), jnp.bfloat16),
            pltpu.SemaphoreType.DMA((2 * tp - 1,)),
            pltpu.SemaphoreType.DMA((2 * tp - 1,)),
        ],
        compiler_params=pltpu.CompilerParams(
            collective_id=1, has_side_effects=True, vmem_limit_bytes=8 * MIB
        ),
    )(part, state)
    return passed[None, None], cache.reshape(1, 1, requests, CTX, lanes)


def solution(mesh):
    in_specs = (
        P("rep", "section", None, None),
        P("section", None),
        P("section", None, "tp"),
        P("rep", "section", None, "tp"),
        P("section", "tp", None),
        P(("rep", "section"), None, "tp"),
        P(("rep", "section"), None, None),
        P(("rep", "section"), None, None),
        P("section"),
        P("rep", "section", None),
    )
    out_specs = (P("rep", "section", None, None), P("rep", "section", None, None, "tp"))
    return jax.shard_map(shards, mesh=mesh, in_specs=in_specs, out_specs=out_specs, check_vma=False)
```

```python
import functools

import jax
import jax.numpy as jnp
from jax import lax
from jax.experimental import pallas as pl
from jax.experimental.pallas import tpu as pltpu
from jax.sharding import PartitionSpec as P

HD = 128
CTX = 512
BLK = 32
MESH = pl.DeviceIdType.MESH
MIB = 2**20
FAR = (1, 3, 2)
CAP_ONE = 42
CAP_TWO = 42
STAY = 128
BALANCE = 0.01


def place():
    rep, section = lax.axis_index("rep"), lax.axis_index("section")
    return (section // 4) * 2 + rep, section % 4, lax.axis_index("tp")


def at(y, z):
    return {"rep": y % 2, "section": (y // 2) * 4 + z}


def group(y, z):
    return (y % 2) * 8 + (y // 2) * 4 + z


def remote(src, dst, send, recv, k, device):
    return pltpu.make_async_remote_copy(
        src_ref=src,
        dst_ref=dst,
        send_sem=send.at[k],
        recv_sem=recv.at[k],
        device_id=device,
        device_id_type=MESH,
    )


def dot(a, b):
    return jnp.dot(a.astype(jnp.bfloat16), b.astype(jnp.bfloat16), preferred_element_type=jnp.float32)


def dot_t(a, b):
    return lax.dot_general(
        a.astype(jnp.bfloat16), b.astype(jnp.bfloat16), (((1,), (1,)), ((), ())), preferred_element_type=jnp.float32
    )


def grid(rows, columns):
    return (
        lax.broadcasted_iota(jnp.int32, (rows, columns), 0),
        lax.broadcasted_iota(jnp.int32, (rows, columns), 1),
    )


def ones(condition):
    return jnp.where(condition, 1.0, 0.0).astype(jnp.float32)


def ring_order(table):
    return jnp.concatenate([table[0:4], table[8:12], table[4:8], table[12:16]], axis=0).astype(jnp.float32)


def widen(table):
    k, lane = grid(32, 128)
    return dot(table, ones(k == lane % 32))


def pack_y(table):
    row, lane = grid(16, 128)
    r, k = grid(8, 16)
    return dot(ones(k // 4 == r), jnp.where(lane // 32 == row % 4, table, 0.0))


def pack_z(table):
    row, lane = grid(16, 128)
    r, k = grid(8, 16)
    return dot(ones((k % 4 == r) & (r < 4)), jnp.where(lane // 32 == row // 4, table, 0.0))


def ranks(valid):
    k, lane = grid(128, 128)
    return dot(valid, ones((k < lane) & (k // 32 == lane // 32)))


def route(masks, y, z):
    flat = masks[...].reshape(128, 128)
    k, lane = grid(128, 128)
    per = dot(flat, ones((k // 32 == lane % 4) & (lane < 16)))
    per = jnp.where((lane // 4 == k % 8) & (lane < 16), per, 0.0)
    g, k = grid(16, 128)
    counts = dot(ones(k // 8 == (g % 4) * 4 + g // 4), per)

    g, h = grid(16, 128)
    inside = h < 16
    off_y = ones((g // 4 != h // 4) & inside)
    off_z = ones((g % 4 != h % 4) & inside)
    a, b = grid(16, 16)
    same_y, same_z = ones(a // 4 == b // 4), ones(a % 4 == b % 4)
    a, b = grid(128, 128)
    both = (a < 16) & (b < 16)
    along_y, along_z = ones((a // 4 == b // 4) & both), ones((a % 4 == b % 4) & both)

    def loads(first, second):
        return (
            dot(same_y, first) * off_y,
            dot(same_z, second) * off_z,
            dot(first, along_z) * off_z,
            dot(second, along_y) * off_y,
        )

    share = jnp.full((16, 128), 0.5, jnp.float32)
    for _ in range(4):
        a1, b1, a2, b2 = loads(counts * share, counts - counts * share)
        share = jnp.clip(share + BALANCE * (jnp.maximum(b1, b2) - jnp.maximum(a1, a2)), 0.0, 1.0)
    share = jnp.where(g == h, 1.0, share)
    first = jnp.floor(counts * share + 0.5)
    second = counts - first
    a1, b1, a2, b2 = loads(first, second)
    over = jnp.maximum(jnp.maximum(a1, b1) - CAP_ONE, jnp.maximum(a2, b2) - CAP_TWO)
    return first, second, jnp.max(over, keepdims=True)


def offsets(first, second):
    a, b = grid(16, 16)
    one_first = dot(ones((a // 4 == b // 4) & (b % 4 < a % 4)), first)
    one_second = dot(ones((a % 4 == b % 4) & (b // 4 < a // 4)), second)
    a, b = grid(128, 128)
    both = (a < 16) & (b < 16)
    two_first = dot(first, ones((a % 4 == b % 4) & (a // 4 < b // 4) & both))
    two_second = dot(second, ones((a // 4 == b // 4) & (a % 4 < b % 4) & both))
    return one_first, one_second, two_first, two_second


def first_tables(masks, index, first, one_first, one_second, y, z, blocks_held):
    flat = masks[...].reshape(128, 128)
    g, k = grid(16, 128)
    mine = dot(ones(k == ((g % 4) * 4 + g // 4) * 8 + y), flat)
    k, lane = grid(128, 128)
    mine = dot(mine, ones(k == z * 32 + lane % 32))
    g, h = grid(16, 128)

    def column(table):
        picked = jnp.sum(jnp.where(h == y * 4 + z, table, 0.0), axis=1, keepdims=True)
        return jnp.broadcast_to(picked, (16, 128))

    taken = column(first)
    place, lane = grid(128, 128)
    row, _ = grid(8, 128)
    out = []
    for pack, start, is_first in ((pack_y, one_first, True), (pack_z, one_second, False)):
        valid = pack(mine)
        rank = ranks(valid)
        limit = pack(taken)
        begin = pack(column(start))
        blocks = pack(index)
        if is_first:
            keep, at_place = (valid > 0.5) & (rank < limit), begin + rank
        else:
            keep, at_place = (valid > 0.5) & (rank >= limit), begin + rank - limit
        at_place = jnp.where(keep, at_place, -1.0)
        table = jnp.zeros((8, 128), jnp.float32)
        for m in range(4):
            hit = ones(at_place[m : m + 1, :].astype(jnp.int32) == place)
            table = jnp.where(row == m, dot_t(blocks, hit), table)
        out.append(table)
    return jnp.clip(jnp.concatenate(out, axis=0).astype(jnp.int32), 0, blocks_held - 1)


def second_tables(first, second, one_first, one_second, two_first, two_second, y, z):
    r, k = grid(8, 16)
    row, lane = grid(8, 128)
    spot = lane.astype(jnp.float32)
    last = STAY + 3 * CAP_ONE - 1
    out = []
    for count, one, two, rows, me, far in (
        (first, one_first, two_first, ones((k == y * 4 + r) & (r < 4)), y, lambda i: i * 4 + z),
        (second, one_second, two_second, ones((k == r * 4 + z) & (r < 4)), z, lambda i: y * 4 + i),
    ):
        count, one, two = dot(rows, count), dot(rows, one), dot(rows, two)
        table = jnp.zeros((8, 128), jnp.float32)
        for i in range(4):
            pick = lane == far(i)
            n = jnp.sum(jnp.where(pick, count, 0.0), axis=1, keepdims=True)
            begin = jnp.sum(jnp.where(pick, one, 0.0), axis=1, keepdims=True)
            shift = jnp.sum(jnp.where(pick, two, 0.0), axis=1, keepdims=True)
            base = part_of((me - i + 4) % 4, CAP_ONE)
            inside = (spot >= shift) & (spot < shift + n)
            table = jnp.where(inside, begin + spot - shift + jnp.full((8, 128), base).astype(jnp.float32), table)
        out.append(table)
    return jnp.clip(jnp.concatenate(out, axis=0).astype(jnp.int32), 0, last)


def part_of(distance, cap):
    return jnp.where(distance == 0, 0, STAY + (distance - 1) * cap)


def final_table(slots, first, two_first, two_second, y, z):
    valid = ones(slots < 255.5)
    rank = ranks(valid)
    r, k = grid(8, 16)
    row, lane = grid(8, 128)
    a, b = grid(128, 128)
    spread = ones((a % 4 == b // 32) & (a < 16))

    def own(table):
        picked = dot(ones(k == y * 4 + z), table)
        return dot(jnp.where((lane // 4 == row) & (lane < 16), picked, 0.0), spread)

    limit, shift_first, shift_second = own(first), own(two_first), own(two_second)
    total = STAY + 3 * CAP_TWO
    base_first = part_of((z - lane // 32 + 4) % 4, CAP_TWO).astype(jnp.float32)
    base_second = (part_of((y - row + 8) % 4, CAP_TWO) + total).astype(jnp.float32)
    spot = jnp.where(rank < limit, base_first + shift_first + rank, base_second + shift_second + rank - limit)
    spot = jnp.clip(spot, 0.0, float(2 * total - 1))
    high = jnp.floor(spot / 16.0)
    low = spot - high * 16.0
    place, _ = grid(256, 128)
    found = jnp.zeros((8, 256), jnp.float32)
    for m in range(4):
        hit = ones(slots[m : m + 1, :].astype(jnp.int32) == place)
        found = found + dot_t(jnp.where(row == m, high, 0.0), hit) * 16.0 + dot_t(jnp.where(row == m, low, 0.0), hit)
    return jnp.clip(jnp.sum(found, axis=0, keepdims=True).astype(jnp.int32), 0, 2 * total - 1)


def move_kernel(
    recv_h, sidx_h, holder, hidden_h, gain_h, pool_h, wq_h, wkv_h,
    fin, q_o, kv_o, inv_o, over_o,
    recv_v, sidx_v, pool, masks, one_v, two_v, one_s, two_s, stage_one, mid, stage_two, wq, wkv, hidden, gain, hpeer,
    kvsend, kvpeer, normed,
    send, recv, side_send, side_recv, mask_send, mask_recv, local,
):
    y, z, _ = place()
    rep = lax.axis_index("rep")
    copies = [
        pltpu.make_async_copy(src, dst, local.at[i])
        for i, (src, dst) in enumerate(
            ((recv_h, recv_v), (sidx_h, sidx_v), (hidden_h, hidden), (pool_h, pool), (gain_h, gain), (wkv_h, wkv), (wq_h, wq))
        )
    ]
    recv_in, sidx_in, hidden_in, pool_in, gain_in, wkv_in, wq_in = copies
    for copy in copies[:5]:
        copy.start()

    barrier = pltpu.get_barrier_semaphore()
    for d in FAR:
        for device in (at((y + d) % 4, z), at(y, (z + d) % 4)):
            pl.semaphore_signal(barrier, inc=1, device_id=device, device_id_type=MESH)

    recv_in.wait()
    row, _ = grid(8, 128)
    slots = jnp.where(row < 4, pack_y(widen(ring_order(recv_v[...]))), 256.0)
    masks[z, y] = ones(slots < 255.5)
    pl.semaphore_wait(barrier, 6)

    hops = []
    for d in FAR:
        copy = remote(masks.at[z, y], masks.at[z, y], mask_send, mask_recv, d - 1, at((y + d) % 4, z))
        copy.start()
        hops.append(copy)
    for copy in hops:
        copy.wait_recv()
    for d in FAR:
        copy = remote(masks.at[z], masks.at[z], mask_send, mask_recv, 3 + d - 1, at(y, (z + d) % 4))
        copy.start()
        hops.append(copy)
    for copy in hops[3:]:
        copy.wait_recv()
    for copy in hops:
        copy.wait_send()

    peer = {"rep": 1 - rep}
    hidden_in.wait()
    to_peer = remote(hidden, hpeer, side_send, side_recv, 0, peer)
    to_peer.start()

    first, second, over = route(masks, y, z)
    one_first, one_second, two_first, two_second = offsets(first, second)
    sidx_in.wait()
    index = widen(ring_order(sidx_v[...]))
    one_v[...] = first_tables(masks, index, first, one_first, one_second, y, z, pool.shape[0])
    one_in = pltpu.make_async_copy(one_v, one_s, local.at[7])
    one_in.start()
    over_o[...] = jnp.broadcast_to(over, over_o.shape).astype(jnp.int32)
    pool_in.wait()
    one_in.wait()

    def pack(dst, begin, count, src, table, line):
        unroll = 8 if count % 8 == 0 else 6

        def body(i, _):
            for u in range(unroll):
                p = i * unroll + u
                dst[begin + p] = src[table[line, p]]
            return 0

        lax.fori_loop(0, count // unroll, body, 0)

    stay_one = STAY + 3 * CAP_ONE
    stay_two = STAY + 3 * CAP_TWO
    started = []
    for d in FAR:
        for way, line, device in ((0, (y + d) % 4, at((y + d) % 4, z)), (1, 8 + (z + d) % 4, at(y, (z + d) % 4))):
            begin = (way * 3 + d - 1) * CAP_ONE
            pack(stage_one, begin, CAP_ONE, pool, one_s, line)
            copy = remote(
                stage_one.at[pl.ds(begin, CAP_ONE)],
                mid.at[way, pl.ds(STAY + (d - 1) * CAP_ONE, CAP_ONE)],
                send, recv, way * 3 + d - 1, device,
            )
            copy.start()
            started.append(copy)
    wkv_in.start()
    wq_in.start()
    pack(mid.at[0], 0, STAY, pool, one_s, y)
    pack(mid.at[1], 0, STAY, pool, one_s, 8 + z)

    two_v[...] = second_tables(first, second, one_first, one_second, two_first, two_second, y, z)
    two_in = pltpu.make_async_copy(two_v, two_s, local.at[8])
    two_in.start()
    inv_o[...] = final_table(slots, first, two_first, two_second, y, z)

    gain_in.wait()
    to_peer.wait_recv()
    width = hidden.shape[1]
    step = 1024
    rows = hidden.shape[0]

    def scale_of(ref):
        total = jnp.zeros((rows, 1), jnp.float32)
        for i in range(width // step):
            part = ref[:, i * step : (i + 1) * step].astype(jnp.float32)
            total = total + jnp.sum(part * part, axis=1, keepdims=True)
        return lax.rsqrt(total / width + 1e-05)

    own_scale, peer_scale = scale_of(hidden), scale_of(hpeer)
    for i in range(width // step):
        cut = slice(i * step, (i + 1) * step)
        g = gain[:, cut]
        normed[0:rows, cut] = (hidden[:, cut].astype(jnp.float32) * own_scale * g).astype(jnp.bfloat16)
        normed[rows : 2 * rows, cut] = (hpeer[:, cut].astype(jnp.float32) * peer_scale * g).astype(jnp.bfloat16)

    def product(count, weight):
        def body(i, total):
            cut = pl.ds(pl.multiple_of(i * step, step), step)
            return total + jnp.dot(normed[0:count, cut], weight[cut, :], preferred_element_type=jnp.float32)

        return lax.fori_loop(0, width // step, body, jnp.zeros((count, weight.shape[1]), jnp.float32))

    wkv_in.wait()
    both = product(2 * rows, wkv).astype(jnp.bfloat16)
    kvsend[...] = both[rows : 2 * rows]
    back = remote(kvsend, kvpeer, side_send, side_recv, 1, peer)
    back.start()
    wq_in.wait()
    query = product(rows, wq).astype(jnp.bfloat16).astype(jnp.float32)
    q_o[...] = jnp.zeros_like(q_o)
    for h in range(query.shape[1] // HD):
        q_o[:, h, :] = query[:, h * HD : (h + 1) * HD]
    back.wait_recv()
    mine = jnp.where(holder[0] == rep, jnp.float32(1), jnp.float32(0))
    own = both[0:rows].astype(jnp.float32)
    other = kvpeer[...].astype(jnp.float32)
    kv_o[...] = jnp.where(jnp.full(own.shape, mine) > 0.5, own, other).astype(jnp.bfloat16)

    two_in.wait()
    for copy in started:
        copy.wait_recv()
    relays = []
    for d in FAR:
        for way, line, device in ((0, (z + d) % 4, at(y, (z + d) % 4)), (1, 8 + (y + d) % 4, at((y + d) % 4, z))):
            begin = STAY + (d - 1) * CAP_TWO
            pack(stage_two.at[way], begin, CAP_TWO, mid.at[way], two_s, line)
            copy = remote(
                stage_two.at[way, pl.ds(begin, CAP_TWO)],
                fin.at[pl.ds(way * stay_two + begin, CAP_TWO)],
                send, recv, 6 + way * 3 + d - 1, device,
            )
            copy.start()
            relays.append(copy)
    keep = []
    for way, line in ((0, z), (1, 8 + y)):
        pack(stage_two.at[way], 0, STAY, mid.at[way], two_s, line)
        copy = pltpu.make_async_copy(
            stage_two.at[way, pl.ds(0, STAY)], fin.at[pl.ds(way * stay_two, STAY)], local.at[9 + way]
        )
        copy.start()
        keep.append(copy)
    for copy in [to_peer, back, *started]:
        copy.wait_send()
    for copy in relays:
        copy.wait_recv()
    for copy in relays:
        copy.wait_send()
    for copy in keep:
        copy.wait()


def whole_kernel(sidx, pool_h, land, pool, stage, send, recv, local):
    y, z, _ = place()
    pool_in = pltpu.make_async_copy(pool_h, pool, local.at[0])
    pool_in.start()
    pairs = [(dy, dz) for dy in range(4) for dz in range(4) if dy or dz]
    barrier = pltpu.get_barrier_semaphore()
    for dy, dz in pairs:
        pl.semaphore_signal(barrier, inc=1, device_id=at((y + dy) % 4, (z + dz) % 4), device_id_type=MESH)
    pl.semaphore_wait(barrier, len(pairs))
    pool_in.wait()
    me = group(y, z)
    copies = []
    for dy, dz in [(0, 0), *pairs]:
        g = group((y + dy) % 4, (z + dz) % 4)
        k = dy * 4 + dz

        def body(c, _):
            stage[k, c] = pool[sidx[g, c]]
            return 0

        lax.fori_loop(0, stage.shape[1], body, 0)
        if k:
            copy = remote(stage.at[k], land.at[me], send, recv, k - 1, at((y + dy) % 4, (z + dz) % 4))
        else:
            copy = pltpu.make_async_copy(stage.at[0], land.at[me], local.at[1])
        copy.start()
        copies.append(copy)
    for copy in copies:
        copy.wait()


def attend_kernel(inv, lengths, land, q, kv, w_h, cache, out, held, w, att, sems):
    w_in = pltpu.make_async_copy(w_h, w, sems.at[0])
    blocks = held.shape[0]

    def fetch(i, _):
        for u in range(8):
            j = i * 8 + u
            pltpu.make_async_copy(land.at[inv[j]], held.at[j], sems.at[1]).start()
        return 0

    lax.fori_loop(0, blocks // 8, fetch, 0)
    w_in.start()
    pltpu.make_async_copy(land.at[pl.ds(0, blocks)], held, sems.at[1]).wait()

    requests = q.shape[0]
    per = blocks // requests
    row = lax.broadcasted_iota(jnp.int32, held.shape[1:], 0)

    for b in range(requests):
        length = lengths[b]
        j = b * per + length // BLK
        held[j] = jnp.where(row == length % BLK, kv[b : b + 1, :].astype(jnp.float32), held[j].astype(jnp.float32)).astype(jnp.bfloat16)
    store = pltpu.make_async_copy(held, cache, sems.at[2])
    store.start()

    position = lax.broadcasted_iota(jnp.int32, (q.shape[1], CTX), 1)

    for b in range(requests):
        keys = held[b * per : (b + 1) * per, :, 0:HD].reshape(CTX, HD)
        values = held[b * per : (b + 1) * per, :, HD : 2 * HD].reshape(CTX, HD)
        scores = lax.dot_general(
            q[b].astype(jnp.bfloat16), keys, (((1,), (1,)), ((), ())), preferred_element_type=jnp.float32
        ) * HD ** (-0.5)
        valid = position <= lengths[b]
        expo = jnp.where(valid, jnp.exp(jnp.where(valid, scores, 0.0)), 0.0)
        weights = (expo / jnp.sum(expo, axis=1, keepdims=True)).astype(jnp.bfloat16)
        att[b] = jnp.dot(weights, values, preferred_element_type=jnp.float32)

    heads = w.shape[0] // HD
    attended = jnp.concatenate([att[:, h, :] for h in range(heads)], axis=1).astype(jnp.bfloat16)
    w_in.wait()
    step = 1024

    def body(i, _):
        cut = pl.ds(pl.multiple_of(i * step, step), step)
        out[:, cut] = jnp.dot(attended, w[:, cut], preferred_element_type=jnp.float32)
        return 0

    lax.fori_loop(0, w.shape[1] // step, body, 0)
    store.wait()


def sum_kernel(part, hidden, out, land, mine, send, recv):
    tp = lax.axis_index("tp")
    section = lax.axis_index("section")
    sections = lax.axis_size("section")
    count = lax.axis_size("tp")
    step = part.shape[1] // count

    def cut(t):
        return pl.ds(pl.multiple_of(t * step, step), step)

    barrier = pltpu.get_barrier_semaphore()
    for k in range(1, count):
        pl.semaphore_signal(barrier, inc=1, device_id={"tp": (tp + k) % count}, device_id_type=MESH)
    before = {"section": (section + sections - 1) % sections}
    pl.semaphore_signal(barrier, inc=1, device_id=before, device_id_type=MESH)
    pl.semaphore_wait(barrier, count)

    sums = []
    for k in range(1, count):
        t = (tp + k) % count
        copy = remote(part.at[:, cut(t)], land.at[k - 1], send, recv, k - 1, {"tp": t})
        copy.start()
        sums.append(copy)
    total = hidden[:, cut(tp)].astype(jnp.float32) + part[:, cut(tp)]
    for k in range(1, count):
        sums[k - 1].wait_recv()
        total = total + land[k - 1]
    mine[...] = total.astype(jnp.bfloat16)
    shift = remote(mine, out.at[:, cut(tp)], send, recv, count - 1, {"section": (section + 1) % sections})
    shift.start()
    shift.wait_recv()
    spread = []
    for k in range(1, count):
        copy = remote(out.at[:, cut(tp)], out.at[:, cut(tp)], send, recv, count + k - 1, {"tp": (tp + k) % count})
        copy.start()
        spread.append(copy)
    for copy in spread:
        copy.wait_recv()
    for copy in [*sums, shift, *spread]:
        copy.wait_send()


def shards(
    hidden, gain, w_query, w_keyval, w_out, old_pool, send_index, recv_slot, holder, lengths
):
    state = hidden[0, 0]
    requests, width = state.shape
    pool_blocks, blk, lanes = old_pool.shape
    groups, cap = send_index.shape[1:]
    blocks = requests * CTX // blk
    heads = w_query.shape[2] // HD
    vmem = pl.BlockSpec(memory_space=pltpu.VMEM)
    smem = pl.BlockSpec(memory_space=pltpu.SMEM)
    hbm = pl.BlockSpec(memory_space=pl.ANY)

    places = 2 * (STAY + 3 * CAP_TWO)
    dma = pltpu.SemaphoreType.DMA
    land, query, keyval, table, over = pl.pallas_call(
        move_kernel,
        name="move",
        out_shape=(
            jax.ShapeDtypeStruct((places, blk, lanes), jnp.bfloat16),
            jax.ShapeDtypeStruct((requests, 8, HD), jnp.float32),
            jax.ShapeDtypeStruct((requests, lanes), jnp.bfloat16),
            jax.ShapeDtypeStruct((1, blocks), jnp.int32),
            jax.ShapeDtypeStruct((8, 128), jnp.int32),
        ),
        in_specs=[hbm, hbm, smem, hbm, hbm, hbm, hbm, hbm],
        out_specs=(hbm, vmem, vmem, vmem, vmem),
        scratch_shapes=[
            pltpu.VMEM((groups, cap), jnp.int32),
            pltpu.VMEM((groups, cap), jnp.int32),
            pltpu.VMEM((pool_blocks, blk, lanes), jnp.bfloat16),
            pltpu.VMEM((4, 4, 8, 128), jnp.float32),
            pltpu.VMEM((16, 128), jnp.int32),
            pltpu.VMEM((16, 128), jnp.int32),
            pltpu.SMEM((16, 128), jnp.int32),
            pltpu.SMEM((16, 128), jnp.int32),
            pltpu.VMEM((6 * CAP_ONE, blk, lanes), jnp.bfloat16),
            pltpu.VMEM((2, STAY + 3 * CAP_ONE, blk, lanes), jnp.bfloat16),
            pltpu.VMEM((2, STAY + 3 * CAP_TWO, blk, lanes), jnp.bfloat16),
            pltpu.VMEM(w_query.shape[1:], jnp.bfloat16),
            pltpu.VMEM(w_keyval.shape[2:], jnp.bfloat16),
            pltpu.VMEM((requests, width), jnp.bfloat16),
            pltpu.VMEM((1, width), jnp.float32),
            pltpu.VMEM((requests, width), jnp.bfloat16),
            pltpu.VMEM((requests, lanes), jnp.bfloat16),
            pltpu.VMEM((requests, lanes), jnp.bfloat16),
            pltpu.VMEM((2 * requests, width), jnp.bfloat16),
            dma((12,)),
            dma((12,)),
            dma((2,)),
            dma((2,)),
            dma((6,)),
            dma((6,)),
            dma((11,)),
        ],
        compiler_params=pltpu.CompilerParams(
            collective_id=0, has_side_effects=True, vmem_limit_bytes=60 * MIB
        ),
    )(recv_slot[0], send_index[0], holder, state, gain, old_pool, w_query[0], w_keyval[0, 0])

    def attend(inverse, held):
        return pl.pallas_call(
            attend_kernel,
            name="attend",
            out_shape=(
                jax.ShapeDtypeStruct((blocks, blk, lanes), jnp.bfloat16),
                jax.ShapeDtypeStruct((requests, width), jnp.float32),
            ),
            in_specs=[smem, smem, hbm, vmem, vmem, hbm],
            out_specs=(hbm, vmem),
            scratch_shapes=[
                pltpu.VMEM((blocks, blk, lanes), jnp.bfloat16),
                pltpu.VMEM(w_out.shape[1:], jnp.bfloat16),
                pltpu.VMEM((requests, 8, HD), jnp.float32),
                dma((3,)),
            ],
            compiler_params=pltpu.CompilerParams(vmem_limit_bytes=60 * MIB),
        )(inverse, lengths[0, 0], held, query, keyval, w_out[0])

    def packed():
        return attend(table[0], land)

    def whole():
        arrived = pl.pallas_call(
            whole_kernel,
            name="whole",
            out_shape=jax.ShapeDtypeStruct((groups, cap, blk, lanes), jnp.bfloat16),
            in_specs=[smem, hbm],
            out_specs=hbm,
            scratch_shapes=[
                pltpu.VMEM((pool_blocks, blk, lanes), jnp.bfloat16),
                pltpu.VMEM((groups, cap, blk, lanes), jnp.bfloat16),
                dma((15,)),
                dma((15,)),
                dma((2,)),
            ],
            compiler_params=pltpu.CompilerParams(
                collective_id=2, has_side_effects=True, vmem_limit_bytes=60 * MIB
            ),
        )(send_index[0], old_pool)
        hit = recv_slot[0].reshape(1, -1) == jnp.arange(blocks, dtype=jnp.int32)[:, None]
        inverse = jnp.sum(jnp.where(hit, jnp.arange(groups * cap, dtype=jnp.int32)[None, :], 0), axis=1)
        return attend(inverse, arrived.reshape(groups * cap, blk, lanes))

    cache, part = lax.cond(over[0, 0] > 0, whole, packed)

    tp = lax.axis_size("tp")
    passed = pl.pallas_call(
        sum_kernel,
        name="sum",
        out_shape=jax.ShapeDtypeStruct((requests, width), jnp.bfloat16),
        in_specs=[vmem, vmem],
        out_specs=vmem,
        scratch_shapes=[
            pltpu.VMEM((tp - 1, requests, width // tp), jnp.float32),
            pltpu.VMEM((requests, width // tp), jnp.bfloat16),
            pltpu.SemaphoreType.DMA((2 * tp - 1,)),
            pltpu.SemaphoreType.DMA((2 * tp - 1,)),
        ],
        compiler_params=pltpu.CompilerParams(
            collective_id=1, has_side_effects=True, vmem_limit_bytes=8 * MIB
        ),
    )(part, state)
    return passed[None, None], cache.reshape(1, 1, requests, CTX, lanes)


def solution(mesh):
    in_specs = (
        P("rep", "section", None, None),
        P("section", None),
        P("section", None, "tp"),
        P("rep", "section", None, "tp"),
        P("section", "tp", None),
        P(("rep", "section"), None, "tp"),
        P(("rep", "section"), None, None),
        P(("rep", "section"), None, None),
        P("section"),
        P("rep", "section", None),
    )
    out_specs = (P("rep", "section", None, None), P("rep", "section", None, None, "tp"))
    return jax.shard_map(shards, mesh=mesh, in_specs=in_specs, out_specs=out_specs, check_vma=False)
```

```python
import functools

import jax
import jax.numpy as jnp
from jax import lax
from jax.experimental import pallas as pl
from jax.experimental.pallas import tpu as pltpu
from jax.sharding import PartitionSpec as P

HD = 128
CTX = 512
BLK = 32
MESH = pl.DeviceIdType.MESH
MIB = 2**20
FAR = (1, 3, 2)
CAP_ONE = 42
CAP_TWO = 42
STAY = 128
BALANCE = 0.01


def place():
    rep, section = lax.axis_index("rep"), lax.axis_index("section")
    return (section // 4) * 2 + rep, section % 4, lax.axis_index("tp")


def at(y, z):
    return {"rep": y % 2, "section": (y // 2) * 4 + z}


def group(y, z):
    return (y % 2) * 8 + (y // 2) * 4 + z


def remote(src, dst, send, recv, k, device):
    return pltpu.make_async_remote_copy(
        src_ref=src,
        dst_ref=dst,
        send_sem=send.at[k],
        recv_sem=recv.at[k],
        device_id=device,
        device_id_type=MESH,
    )


def dot(a, b):
    return jnp.dot(a.astype(jnp.bfloat16), b.astype(jnp.bfloat16), preferred_element_type=jnp.float32)


def dot_t(a, b):
    return lax.dot_general(
        a.astype(jnp.bfloat16), b.astype(jnp.bfloat16), (((1,), (1,)), ((), ())), preferred_element_type=jnp.float32
    )


def grid(rows, columns):
    return (
        lax.broadcasted_iota(jnp.int32, (rows, columns), 0),
        lax.broadcasted_iota(jnp.int32, (rows, columns), 1),
    )


def ones(condition):
    return jnp.where(condition, 1.0, 0.0).astype(jnp.float32)


def ring_order(table):
    return jnp.concatenate([table[0:4], table[8:12], table[4:8], table[12:16]], axis=0).astype(jnp.float32)


def widen(table):
    k, lane = grid(32, 128)
    return dot(table, ones(k == lane % 32))


def pack_y(table):
    row, lane = grid(16, 128)
    r, k = grid(8, 16)
    return dot(ones(k // 4 == r), jnp.where(lane // 32 == row % 4, table, 0.0))


def pack_z(table):
    row, lane = grid(16, 128)
    r, k = grid(8, 16)
    return dot(ones((k % 4 == r) & (r < 4)), jnp.where(lane // 32 == row // 4, table, 0.0))


def ranks(valid):
    k, lane = grid(128, 128)
    return dot(valid, ones((k < lane) & (k // 32 == lane // 32)))


def route(masks, y, z):
    flat = masks[...].reshape(128, 128)
    k, lane = grid(128, 128)
    per = dot(flat, ones((k // 32 == lane % 4) & (lane < 16)))
    per = jnp.where((lane // 4 == k % 8) & (lane < 16), per, 0.0)
    g, k = grid(16, 128)
    counts = dot(ones(k // 8 == (g % 4) * 4 + g // 4), per)

    g, h = grid(16, 128)
    inside = h < 16
    off_y = ones((g // 4 != h // 4) & inside)
    off_z = ones((g % 4 != h % 4) & inside)
    a, b = grid(16, 16)
    same_y, same_z = ones(a // 4 == b // 4), ones(a % 4 == b % 4)
    a, b = grid(128, 128)
    both = (a < 16) & (b < 16)
    along_y, along_z = ones((a // 4 == b // 4) & both), ones((a % 4 == b % 4) & both)

    def loads(first, second):
        return (
            dot(same_y, first) * off_y,
            dot(same_z, second) * off_z,
            dot(first, along_z) * off_z,
            dot(second, along_y) * off_y,
        )

    share = jnp.full((16, 128), 0.5, jnp.float32)
    for _ in range(4):
        a1, b1, a2, b2 = loads(counts * share, counts - counts * share)
        share = jnp.clip(share + BALANCE * (jnp.maximum(b1, b2) - jnp.maximum(a1, a2)), 0.0, 1.0)
    share = jnp.where(g == h, 1.0, share)
    first = jnp.floor(counts * share + 0.5)
    second = counts - first
    a1, b1, a2, b2 = loads(first, second)
    over = jnp.maximum(jnp.maximum(a1, b1) - CAP_ONE, jnp.maximum(a2, b2) - CAP_TWO)
    return first, second, jnp.max(over, keepdims=True)


def offsets(first, second):
    a, b = grid(16, 16)
    one_first = dot(ones((a // 4 == b // 4) & (b % 4 < a % 4)), first)
    one_second = dot(ones((a % 4 == b % 4) & (b // 4 < a // 4)), second)
    a, b = grid(128, 128)
    both = (a < 16) & (b < 16)
    two_first = dot(first, ones((a % 4 == b % 4) & (a // 4 < b // 4) & both))
    two_second = dot(second, ones((a // 4 == b // 4) & (a % 4 < b % 4) & both))
    return one_first, one_second, two_first, two_second


def first_tables(masks, index, first, one_first, one_second, y, z, blocks_held):
    flat = masks[...].reshape(128, 128)
    g, k = grid(16, 128)
    mine = dot(ones(k == ((g % 4) * 4 + g // 4) * 8 + y), flat)
    k, lane = grid(128, 128)
    mine = dot(mine, ones(k == z * 32 + lane % 32))
    g, h = grid(16, 128)

    def column(table):
        picked = jnp.sum(jnp.where(h == y * 4 + z, table, 0.0), axis=1, keepdims=True)
        return jnp.broadcast_to(picked, (16, 128))

    taken = column(first)
    place, lane = grid(128, 128)
    row, _ = grid(8, 128)
    out = []
    for pack, start, is_first in ((pack_y, one_first, True), (pack_z, one_second, False)):
        valid = pack(mine)
        rank = ranks(valid)
        limit = pack(taken)
        begin = pack(column(start))
        blocks = pack(index)
        if is_first:
            keep, at_place = (valid > 0.5) & (rank < limit), begin + rank
        else:
            keep, at_place = (valid > 0.5) & (rank >= limit), begin + rank - limit
        at_place = jnp.where(keep, at_place, -1.0)
        table = jnp.zeros((8, 128), jnp.float32)
        for m in range(4):
            hit = ones(at_place[m : m + 1, :].astype(jnp.int32) == place)
            table = jnp.where(row == m, dot_t(blocks, hit), table)
        out.append(table)
    return jnp.clip(jnp.concatenate(out, axis=0).astype(jnp.int32), 0, blocks_held - 1)


def second_tables(first, second, one_first, one_second, two_first, two_second, y, z):
    r, k = grid(8, 16)
    row, lane = grid(8, 128)
    spot = lane.astype(jnp.float32)
    last = STAY + 3 * CAP_ONE - 1
    out = []
    for count, one, two, rows, me, far in (
        (first, one_first, two_first, ones((k == y * 4 + r) & (r < 4)), y, lambda i: i * 4 + z),
        (second, one_second, two_second, ones((k == r * 4 + z) & (r < 4)), z, lambda i: y * 4 + i),
    ):
        count, one, two = dot(rows, count), dot(rows, one), dot(rows, two)
        table = jnp.zeros((8, 128), jnp.float32)
        for i in range(4):
            pick = lane == far(i)
            n = jnp.sum(jnp.where(pick, count, 0.0), axis=1, keepdims=True)
            begin = jnp.sum(jnp.where(pick, one, 0.0), axis=1, keepdims=True)
            shift = jnp.sum(jnp.where(pick, two, 0.0), axis=1, keepdims=True)
            base = part_of((me - i + 4) % 4, CAP_ONE)
            inside = (spot >= shift) & (spot < shift + n)
            table = jnp.where(inside, begin + spot - shift + jnp.full((8, 128), base).astype(jnp.float32), table)
        out.append(table)
    return jnp.clip(jnp.concatenate(out, axis=0).astype(jnp.int32), 0, last)


def part_of(distance, cap):
    return jnp.where(distance == 0, 0, STAY + (distance - 1) * cap)


def final_table(slots, first, two_first, two_second, y, z):
    valid = ones(slots < 255.5)
    rank = ranks(valid)
    r, k = grid(8, 16)
    row, lane = grid(8, 128)
    a, b = grid(128, 128)
    spread = ones((a % 4 == b // 32) & (a < 16))

    def own(table):
        picked = dot(ones(k == y * 4 + z), table)
        return dot(jnp.where((lane // 4 == row) & (lane < 16), picked, 0.0), spread)

    limit, shift_first, shift_second = own(first), own(two_first), own(two_second)
    total = STAY + 3 * CAP_TWO
    base_first = part_of((z - lane // 32 + 4) % 4, CAP_TWO).astype(jnp.float32)
    base_second = (part_of((y - row + 8) % 4, CAP_TWO) + total).astype(jnp.float32)
    spot = jnp.where(rank < limit, base_first + shift_first + rank, base_second + shift_second + rank - limit)
    spot = jnp.clip(spot, 0.0, float(2 * total - 1))
    high = jnp.floor(spot / 16.0)
    low = spot - high * 16.0
    place, _ = grid(256, 128)
    found = jnp.zeros((8, 256), jnp.float32)
    for m in range(4):
        hit = ones(slots[m : m + 1, :].astype(jnp.int32) == place)
        found = found + dot_t(jnp.where(row == m, high, 0.0), hit) * 16.0 + dot_t(jnp.where(row == m, low, 0.0), hit)
    return jnp.clip(jnp.sum(found, axis=0, keepdims=True).astype(jnp.int32), 0, 2 * total - 1)


def move_kernel(
    recv_h, sidx_h, holder, hidden_h, gain_h, pool_h, wq_h, wkv_h,
    fin, q_o, kv_o, inv_o, over_o,
    recv_v, sidx_v, pool, masks, one_v, two_v, one_s, two_s, stage_one, mid, stage_two, wq, wkv, hidden, gain, hpeer,
    kvsend, kvpeer, normed,
    send, recv, side_send, side_recv, mask_send, mask_recv, local,
):
    y, z, tp = place()
    rep = lax.axis_index("rep")
    count = lax.axis_size("tp")
    copies = [
        pltpu.make_async_copy(src, dst, local.at[i])
        for i, (src, dst) in enumerate(
            ((recv_h, recv_v), (sidx_h, sidx_v), (hidden_h, hidden), (pool_h, pool), (gain_h, gain), (wkv_h, wkv), (wq_h, wq))
        )
    ]
    recv_in, sidx_in, hidden_in, pool_in, gain_in, wkv_in, wq_in = copies
    for copy in copies[:5]:
        copy.start()

    barrier = pltpu.get_barrier_semaphore()
    for d in FAR:
        for device in (at((y + d) % 4, z), at(y, (z + d) % 4)):
            pl.semaphore_signal(barrier, inc=1, device_id=device, device_id_type=MESH)
    for k in range(1, count):
        pl.semaphore_signal(barrier, inc=1, device_id={"tp": (tp + k) % count}, device_id_type=MESH)

    recv_in.wait()
    row, _ = grid(8, 128)
    slots = jnp.where(row < 4, pack_y(widen(ring_order(recv_v[...]))), 256.0)
    masks[z, y] = ones(slots < 255.5)
    pl.semaphore_wait(barrier, 6 + count - 1)

    hops = []
    for d in FAR:
        copy = remote(masks.at[z, y], masks.at[z, y], mask_send, mask_recv, d - 1, at((y + d) % 4, z))
        copy.start()
        hops.append(copy)
    for copy in hops:
        copy.wait_recv()
    for d in FAR:
        copy = remote(masks.at[z], masks.at[z], mask_send, mask_recv, 3 + d - 1, at(y, (z + d) % 4))
        copy.start()
        hops.append(copy)
    for copy in hops[3:]:
        copy.wait_recv()
    for copy in hops:
        copy.wait_send()

    peer = {"rep": 1 - rep}
    hidden_in.wait()
    share = hidden.shape[1] // count
    eighth = pl.ds(pl.multiple_of(tp * share, share), share)
    to_peer = remote(hidden.at[:, eighth], hpeer.at[:, eighth], side_send, side_recv, 0, peer)
    to_peer.start()

    first, second, over = route(masks, y, z)
    one_first, one_second, two_first, two_second = offsets(first, second)
    sidx_in.wait()
    index = widen(ring_order(sidx_v[...]))
    table = first_tables(masks, index, first, one_first, one_second, y, z, pool.shape[0])
    row, _ = grid(16, 128)
    one_v[...] = jnp.where(row == 4, jnp.broadcast_to(over, (16, 128)).astype(jnp.int32), table)
    one_in = pltpu.make_async_copy(one_v, one_s, local.at[7])
    one_in.start()
    pool_in.wait()
    one_in.wait()
    over_o[0] = one_s[4, 0]

    def pack(dst, begin, count, src, table, line):
        unroll = 8 if count % 8 == 0 else 6

        def body(i, _):
            for u in range(unroll):
                p = i * unroll + u
                dst[begin + p] = src[table[line, p]]
            return 0

        lax.fori_loop(0, count // unroll, body, 0)

    stay_one = STAY + 3 * CAP_ONE
    stay_two = STAY + 3 * CAP_TWO
    started = []
    for d in FAR:
        for way, line, device in ((0, (y + d) % 4, at((y + d) % 4, z)), (1, 8 + (z + d) % 4, at(y, (z + d) % 4))):
            begin = (way * 3 + d - 1) * CAP_ONE
            pack(stage_one, begin, CAP_ONE, pool, one_s, line)
            copy = remote(
                stage_one.at[pl.ds(begin, CAP_ONE)],
                mid.at[way, pl.ds(STAY + (d - 1) * CAP_ONE, CAP_ONE)],
                send, recv, way * 3 + d - 1, device,
            )
            copy.start()
            started.append(copy)
    wkv_in.start()
    wq_in.start()
    to_peer.wait_recv()
    shared = []
    for k in range(1, count):
        copy = remote(
            hpeer.at[:, eighth], hpeer.at[:, eighth], side_send, side_recv, 1 + k, {"tp": (tp + k) % count}
        )
        copy.start()
        shared.append(copy)
    pack(mid.at[0], 0, STAY, pool, one_s, y)
    pack(mid.at[1], 0, STAY, pool, one_s, 8 + z)

    two_v[...] = second_tables(first, second, one_first, one_second, two_first, two_second, y, z)
    two_in = pltpu.make_async_copy(two_v, two_s, local.at[8])
    two_in.start()
    inv_o[...] = final_table(slots, first, two_first, two_second, y, z)

    gain_in.wait()
    for copy in shared:
        copy.wait_recv()
    width = hidden.shape[1]
    step = 1024
    rows = hidden.shape[0]

    def scale_of(ref):
        total = jnp.zeros((rows, 1), jnp.float32)
        for i in range(width // step):
            part = ref[:, i * step : (i + 1) * step].astype(jnp.float32)
            total = total + jnp.sum(part * part, axis=1, keepdims=True)
        return lax.rsqrt(total / width + 1e-05)

    own_scale, peer_scale = scale_of(hidden), scale_of(hpeer)
    for i in range(width // step):
        cut = slice(i * step, (i + 1) * step)
        g = gain[:, cut]
        normed[0:rows, cut] = (hidden[:, cut].astype(jnp.float32) * own_scale * g).astype(jnp.bfloat16)
        normed[rows : 2 * rows, cut] = (hpeer[:, cut].astype(jnp.float32) * peer_scale * g).astype(jnp.bfloat16)

    def product(count, weight):
        def body(i, total):
            cut = pl.ds(pl.multiple_of(i * step, step), step)
            return total + jnp.dot(normed[0:count, cut], weight[cut, :], preferred_element_type=jnp.float32)

        return lax.fori_loop(0, width // step, body, jnp.zeros((count, weight.shape[1]), jnp.float32))

    wkv_in.wait()
    both = product(2 * rows, wkv).astype(jnp.bfloat16)
    kvsend[...] = both[rows : 2 * rows]
    back = remote(kvsend, kvpeer, side_send, side_recv, 1, peer)
    back.start()
    wq_in.wait()
    query = product(rows, wq).astype(jnp.bfloat16).astype(jnp.float32)
    q_o[...] = jnp.zeros_like(q_o)
    for h in range(query.shape[1] // HD):
        q_o[:, h, :] = query[:, h * HD : (h + 1) * HD]
    back.wait_recv()
    mine = jnp.where(holder[0] == rep, jnp.float32(1), jnp.float32(0))
    own = both[0:rows].astype(jnp.float32)
    other = kvpeer[...].astype(jnp.float32)
    kv_o[...] = jnp.where(jnp.full(own.shape, mine) > 0.5, own, other).astype(jnp.bfloat16)

    two_in.wait()
    for copy in started:
        copy.wait_recv()
    relays = []
    for d in FAR:
        for way, line, device in ((0, (z + d) % 4, at(y, (z + d) % 4)), (1, 8 + (y + d) % 4, at((y + d) % 4, z))):
            begin = STAY + (d - 1) * CAP_TWO
            pack(stage_two.at[way], begin, CAP_TWO, mid.at[way], two_s, line)
            copy = remote(
                stage_two.at[way, pl.ds(begin, CAP_TWO)],
                fin.at[pl.ds(way * stay_two + begin, CAP_TWO)],
                send, recv, 6 + way * 3 + d - 1, device,
            )
            copy.start()
            relays.append(copy)
    keep = []
    for way, line in ((0, z), (1, 8 + y)):
        pack(stage_two.at[way], 0, STAY, mid.at[way], two_s, line)
        copy = pltpu.make_async_copy(
            stage_two.at[way, pl.ds(0, STAY)], fin.at[pl.ds(way * stay_two, STAY)], local.at[9 + way]
        )
        copy.start()
        keep.append(copy)
    for copy in [to_peer, back, *shared, *started]:
        copy.wait_send()
    for copy in relays:
        copy.wait_recv()
    for copy in relays:
        copy.wait_send()
    for copy in keep:
        copy.wait()


def whole_kernel(sidx, pool_h, land, pool, stage, send, recv, local):
    y, z, _ = place()
    pool_in = pltpu.make_async_copy(pool_h, pool, local.at[0])
    pool_in.start()
    pairs = [(dy, dz) for dy in range(4) for dz in range(4) if dy or dz]
    barrier = pltpu.get_barrier_semaphore()
    for dy, dz in pairs:
        pl.semaphore_signal(barrier, inc=1, device_id=at((y + dy) % 4, (z + dz) % 4), device_id_type=MESH)
    pl.semaphore_wait(barrier, len(pairs))
    pool_in.wait()
    me = group(y, z)
    copies = []
    for dy, dz in [(0, 0), *pairs]:
        g = group((y + dy) % 4, (z + dz) % 4)
        k = dy * 4 + dz

        def body(c, _):
            stage[k, c] = pool[sidx[g, c]]
            return 0

        lax.fori_loop(0, stage.shape[1], body, 0)
        if k:
            copy = remote(stage.at[k], land.at[me], send, recv, k - 1, at((y + dy) % 4, (z + dz) % 4))
        else:
            copy = pltpu.make_async_copy(stage.at[0], land.at[me], local.at[1])
        copy.start()
        copies.append(copy)
    for copy in copies:
        copy.wait()


def attend_kernel(inv, lengths, land, q, kv, cache, out, held, att, ready, stored):
    requests = q.shape[0]
    per = held.shape[0] // requests

    def part(b):
        return pl.ds(b * per, per)

    def fetch(b, _):
        for u in range(per):
            j = b * per + u
            pltpu.make_async_copy(land.at[inv[j]], held.at[j], ready.at[b]).start()
        return 0

    lax.fori_loop(0, requests, fetch, 0)

    row = lax.broadcasted_iota(jnp.int32, held.shape[1:], 0)
    position = lax.broadcasted_iota(jnp.int32, (q.shape[1], CTX), 1)
    stores = []
    for b in range(requests):
        pltpu.make_async_copy(land.at[pl.ds(0, per)], held.at[part(b)], ready.at[b]).wait()
        length = lengths[b]
        j = b * per + length // BLK
        fresh = jnp.broadcast_to(kv[b : b + 1, :].astype(jnp.float32), row.shape)
        held[j] = jnp.where(row == length % BLK, fresh, held[j].astype(jnp.float32)).astype(jnp.bfloat16)
        store = pltpu.make_async_copy(held.at[part(b)], cache.at[part(b)], stored.at[b])
        store.start()
        stores.append(store)
        keys = held[b * per : (b + 1) * per, :, 0:HD].reshape(CTX, HD)
        values = held[b * per : (b + 1) * per, :, HD : 2 * HD].reshape(CTX, HD)
        scores = lax.dot_general(
            q[b].astype(jnp.bfloat16), keys, (((1,), (1,)), ((), ())), preferred_element_type=jnp.float32
        ) * HD ** (-0.5)
        valid = position <= length
        expo = jnp.where(valid, jnp.exp(jnp.where(valid, scores, 0.0)), 0.0)
        weights = (expo / jnp.sum(expo, axis=1, keepdims=True)).astype(jnp.bfloat16)
        att[b] = jnp.dot(weights, values, preferred_element_type=jnp.float32)

    heads = out.shape[1] // HD
    out[...] = jnp.concatenate([att[:, h, :] for h in range(heads)], axis=1).astype(jnp.bfloat16)
    for store in stores:
        store.wait()


def finish_kernel(attended, hidden, w_h, out, w, part, land, mine, send, recv, loaded):
    tp = lax.axis_index("tp")
    section = lax.axis_index("section")
    sections = lax.axis_size("section")
    count = lax.axis_size("tp")
    step = out.shape[1] // count

    def cut(t):
        return pl.ds(pl.multiple_of(t * step, step), step)

    order = [*range(1, count), 0]
    loads = {}
    for k in order:
        loads[k] = pltpu.make_async_copy(w_h.at[:, cut((tp + k) % count)], w.at[k], loaded.at[k])
        loads[k].start()

    barrier = pltpu.get_barrier_semaphore()
    for k in range(1, count):
        pl.semaphore_signal(barrier, inc=1, device_id={"tp": (tp + k) % count}, device_id_type=MESH)
    before = {"section": (section + sections - 1) % sections}
    pl.semaphore_signal(barrier, inc=1, device_id=before, device_id_type=MESH)

    sums = []
    for k in order:
        loads[k].wait()
        chunk = jnp.dot(attended[...], w[k], preferred_element_type=jnp.float32)
        if k:
            part[k - 1] = chunk.astype(jnp.bfloat16)
            if not sums:
                pl.semaphore_wait(barrier, count)
            copy = remote(part.at[k - 1], land.at[k - 1], send, recv, k - 1, {"tp": (tp + k) % count})
            copy.start()
            sums.append(copy)
    total = hidden[:, cut(tp)].astype(jnp.float32) + chunk
    for k in range(1, count):
        sums[k - 1].wait_recv()
        total = total + land[k - 1].astype(jnp.float32)
    mine[...] = total.astype(jnp.bfloat16)
    shift = remote(mine, out.at[:, cut(tp)], send, recv, count - 1, {"section": (section + 1) % sections})
    shift.start()
    shift.wait_recv()
    spread = []
    for k in range(1, count):
        copy = remote(out.at[:, cut(tp)], out.at[:, cut(tp)], send, recv, count + k - 1, {"tp": (tp + k) % count})
        copy.start()
        spread.append(copy)
    for copy in spread:
        copy.wait_recv()
    for copy in [*sums, shift, *spread]:
        copy.wait_send()


def shards(
    hidden, gain, w_query, w_keyval, w_out, old_pool, send_index, recv_slot, holder, lengths
):
    state = hidden[0, 0]
    requests, width = state.shape
    pool_blocks, blk, lanes = old_pool.shape
    groups, cap = send_index.shape[1:]
    blocks = requests * CTX // blk
    heads = w_query.shape[2] // HD
    vmem = pl.BlockSpec(memory_space=pltpu.VMEM)
    smem = pl.BlockSpec(memory_space=pltpu.SMEM)
    hbm = pl.BlockSpec(memory_space=pl.ANY)

    tp = lax.axis_size("tp")
    places = 2 * (STAY + 3 * CAP_TWO)
    dma = pltpu.SemaphoreType.DMA
    land, query, keyval, table, over = pl.pallas_call(
        move_kernel,
        name="move",
        out_shape=(
            jax.ShapeDtypeStruct((places, blk, lanes), jnp.bfloat16),
            jax.ShapeDtypeStruct((requests, 8, HD), jnp.float32),
            jax.ShapeDtypeStruct((requests, lanes), jnp.bfloat16),
            jax.ShapeDtypeStruct((1, blocks), jnp.int32),
            jax.ShapeDtypeStruct((1,), jnp.int32),
        ),
        in_specs=[hbm, hbm, smem, hbm, hbm, hbm, hbm, hbm],
        out_specs=(hbm, vmem, vmem, vmem, smem),
        scratch_shapes=[
            pltpu.VMEM((groups, cap), jnp.int32),
            pltpu.VMEM((groups, cap), jnp.int32),
            pltpu.VMEM((pool_blocks, blk, lanes), jnp.bfloat16),
            pltpu.VMEM((4, 4, 8, 128), jnp.float32),
            pltpu.VMEM((16, 128), jnp.int32),
            pltpu.VMEM((16, 128), jnp.int32),
            pltpu.SMEM((16, 128), jnp.int32),
            pltpu.SMEM((16, 128), jnp.int32),
            pltpu.VMEM((6 * CAP_ONE, blk, lanes), jnp.bfloat16),
            pltpu.VMEM((2, STAY + 3 * CAP_ONE, blk, lanes), jnp.bfloat16),
            pltpu.VMEM((2, STAY + 3 * CAP_TWO, blk, lanes), jnp.bfloat16),
            pltpu.VMEM(w_query.shape[1:], jnp.bfloat16),
            pltpu.VMEM(w_keyval.shape[2:], jnp.bfloat16),
            pltpu.VMEM((requests, width), jnp.bfloat16),
            pltpu.VMEM((1, width), jnp.float32),
            pltpu.VMEM((requests, width), jnp.bfloat16),
            pltpu.VMEM((requests, lanes), jnp.bfloat16),
            pltpu.VMEM((requests, lanes), jnp.bfloat16),
            pltpu.VMEM((2 * requests, width), jnp.bfloat16),
            dma((12,)),
            dma((12,)),
            dma((tp + 1,)),
            dma((tp + 1,)),
            dma((6,)),
            dma((6,)),
            dma((11,)),
        ],
        compiler_params=pltpu.CompilerParams(
            collective_id=0, has_side_effects=True, vmem_limit_bytes=60 * MIB
        ),
    )(recv_slot[0], send_index[0], holder, state, gain, old_pool, w_query[0], w_keyval[0, 0])

    def attend(inverse, held):
        return pl.pallas_call(
            attend_kernel,
            name="attend",
            out_shape=(
                jax.ShapeDtypeStruct((blocks, blk, lanes), jnp.bfloat16),
                jax.ShapeDtypeStruct((requests, heads * HD), jnp.bfloat16),
            ),
            in_specs=[smem, smem, hbm, vmem, vmem],
            out_specs=(hbm, vmem),
            scratch_shapes=[
                pltpu.VMEM((blocks, blk, lanes), jnp.bfloat16),
                pltpu.VMEM((requests, 8, HD), jnp.float32),
                dma((requests,)),
                dma((requests,)),
            ],
            compiler_params=pltpu.CompilerParams(vmem_limit_bytes=60 * MIB),
        )(inverse, lengths[0, 0], held, query, keyval)

    def packed():
        return attend(table[0], land)

    def whole():
        arrived = pl.pallas_call(
            whole_kernel,
            name="whole",
            out_shape=jax.ShapeDtypeStruct((groups, cap, blk, lanes), jnp.bfloat16),
            in_specs=[smem, hbm],
            out_specs=hbm,
            scratch_shapes=[
                pltpu.VMEM((pool_blocks, blk, lanes), jnp.bfloat16),
                pltpu.VMEM((groups, cap, blk, lanes), jnp.bfloat16),
                dma((15,)),
                dma((15,)),
                dma((2,)),
            ],
            compiler_params=pltpu.CompilerParams(
                collective_id=2, has_side_effects=True, vmem_limit_bytes=60 * MIB
            ),
        )(send_index[0], old_pool)
        hit = recv_slot[0].reshape(1, -1) == jnp.arange(blocks, dtype=jnp.int32)[:, None]
        inverse = jnp.sum(jnp.where(hit, jnp.arange(groups * cap, dtype=jnp.int32)[None, :], 0), axis=1)
        return attend(inverse, arrived.reshape(groups * cap, blk, lanes))

    cache, attended = lax.cond(over[0] > 0, whole, packed)

    passed = pl.pallas_call(
        finish_kernel,
        name="finish",
        out_shape=jax.ShapeDtypeStruct((requests, width), jnp.bfloat16),
        in_specs=[vmem, vmem, hbm],
        out_specs=vmem,
        scratch_shapes=[
            pltpu.VMEM((tp, heads * HD, width // tp), jnp.bfloat16),
            pltpu.VMEM((tp - 1, requests, width // tp), jnp.bfloat16),
            pltpu.VMEM((tp - 1, requests, width // tp), jnp.bfloat16),
            pltpu.VMEM((requests, width // tp), jnp.bfloat16),
            dma((2 * tp - 1,)),
            dma((2 * tp - 1,)),
            dma((tp,)),
        ],
        compiler_params=pltpu.CompilerParams(
            collective_id=1, has_side_effects=True, vmem_limit_bytes=60 * MIB
        ),
    )(attended, state, w_out[0])
    return passed[None, None], cache.reshape(1, 1, requests, CTX, lanes)


def solution(mesh):
    in_specs = (
        P("rep", "section", None, None),
        P("section", None),
        P("section", None, "tp"),
        P("rep", "section", None, "tp"),
        P("section", "tp", None),
        P(("rep", "section"), None, "tp"),
        P(("rep", "section"), None, None),
        P(("rep", "section"), None, None),
        P("section"),
        P("rep", "section", None),
    )
    out_specs = (P("rep", "section", None, None), P("rep", "section", None, None, "tp"))
    return jax.shard_map(shards, mesh=mesh, in_specs=in_specs, out_specs=out_specs, check_vma=False)
```

```python
import functools

import jax
import jax.numpy as jnp
from jax import lax
from jax.experimental import pallas as pl
from jax.experimental.pallas import tpu as pltpu
from jax.sharding import PartitionSpec as P

HD = 128
CTX = 512
BLK = 32
MESH = pl.DeviceIdType.MESH
MIB = 2**20
FAR = (1, 3, 2)
CAP_ONE = 41
CAP_TWO = 41
STAY = 128
BALANCE = 0.01


def place():
    rep, section = lax.axis_index("rep"), lax.axis_index("section")
    return (section // 4) * 2 + rep, section % 4, lax.axis_index("tp")


def at(y, z):
    return {"rep": y % 2, "section": (y // 2) * 4 + z}


def group(y, z):
    return (y % 2) * 8 + (y // 2) * 4 + z


def remote(src, dst, send, recv, k, device):
    return pltpu.make_async_remote_copy(
        src_ref=src,
        dst_ref=dst,
        send_sem=send.at[k],
        recv_sem=recv.at[k],
        device_id=device,
        device_id_type=MESH,
    )


def dot(a, b):
    return jnp.dot(a.astype(jnp.bfloat16), b.astype(jnp.bfloat16), preferred_element_type=jnp.float32)


def dot_t(a, b):
    return lax.dot_general(
        a.astype(jnp.bfloat16), b.astype(jnp.bfloat16), (((1,), (1,)), ((), ())), preferred_element_type=jnp.float32
    )


def grid(rows, columns):
    return (
        lax.broadcasted_iota(jnp.int32, (rows, columns), 0),
        lax.broadcasted_iota(jnp.int32, (rows, columns), 1),
    )


def ones(condition):
    return jnp.where(condition, 1.0, 0.0).astype(jnp.float32)


def ring_order(table):
    return jnp.concatenate([table[0:4], table[8:12], table[4:8], table[12:16]], axis=0).astype(jnp.float32)


def widen(table):
    k, lane = grid(32, 128)
    return dot(table, ones(k == lane % 32))


def pack_y(table):
    row, lane = grid(16, 128)
    r, k = grid(8, 16)
    return dot(ones(k // 4 == r), jnp.where(lane // 32 == row % 4, table, 0.0))


def pack_z(table):
    row, lane = grid(16, 128)
    r, k = grid(8, 16)
    return dot(ones((k % 4 == r) & (r < 4)), jnp.where(lane // 32 == row // 4, table, 0.0))


def ranks(valid):
    k, lane = grid(128, 128)
    return dot(valid, ones((k < lane) & (k // 32 == lane // 32)))


def route(masks, y, z):
    flat = masks[...].reshape(128, 128)
    k, lane = grid(128, 128)
    per = dot(flat, ones((k // 32 == lane % 4) & (lane < 16)))
    per = jnp.where((lane // 4 == k % 8) & (lane < 16), per, 0.0)
    g, k = grid(16, 128)
    counts = dot(ones(k // 8 == (g % 4) * 4 + g // 4), per)

    g, h = grid(16, 128)
    inside = h < 16
    off_y = ones((g // 4 != h // 4) & inside)
    off_z = ones((g % 4 != h % 4) & inside)
    a, b = grid(16, 16)
    same_y, same_z = ones(a // 4 == b // 4), ones(a % 4 == b % 4)
    a, b = grid(128, 128)
    both = (a < 16) & (b < 16)
    along_y, along_z = ones((a // 4 == b // 4) & both), ones((a % 4 == b % 4) & both)

    def loads(first, second):
        return (
            dot(same_y, first) * off_y,
            dot(same_z, second) * off_z,
            dot(first, along_z) * off_z,
            dot(second, along_y) * off_y,
        )

    share = jnp.full((16, 128), 0.5, jnp.float32)
    for _ in range(4):
        a1, b1, a2, b2 = loads(counts * share, counts - counts * share)
        share = jnp.clip(share + BALANCE * (jnp.maximum(b1, b2) - jnp.maximum(a1, a2)), 0.0, 1.0)
    share = jnp.where(g == h, 1.0, share)
    first = jnp.floor(counts * share + 0.5)
    second = counts - first
    a1, b1, a2, b2 = loads(first, second)
    over = jnp.maximum(jnp.maximum(a1, b1) - CAP_ONE, jnp.maximum(a2, b2) - CAP_TWO)
    return first, second, jnp.max(over, keepdims=True)


def offsets(first, second):
    a, b = grid(16, 16)
    one_first = dot(ones((a // 4 == b // 4) & (b % 4 < a % 4)), first)
    one_second = dot(ones((a % 4 == b % 4) & (b // 4 < a // 4)), second)
    a, b = grid(128, 128)
    both = (a < 16) & (b < 16)
    two_first = dot(first, ones((a % 4 == b % 4) & (a // 4 < b // 4) & both))
    two_second = dot(second, ones((a // 4 == b // 4) & (a % 4 < b % 4) & both))
    return one_first, one_second, two_first, two_second


def first_tables(masks, index, first, one_first, one_second, y, z, blocks_held):
    flat = masks[...].reshape(128, 128)
    g, k = grid(16, 128)
    mine = dot(ones(k == ((g % 4) * 4 + g // 4) * 8 + y), flat)
    k, lane = grid(128, 128)
    mine = dot(mine, ones(k == z * 32 + lane % 32))
    g, h = grid(16, 128)

    def column(table):
        picked = jnp.sum(jnp.where(h == y * 4 + z, table, 0.0), axis=1, keepdims=True)
        return jnp.broadcast_to(picked, (16, 128))

    taken = column(first)
    place, lane = grid(128, 128)
    row, _ = grid(8, 128)
    out = []
    for pack, start, is_first in ((pack_y, one_first, True), (pack_z, one_second, False)):
        valid = pack(mine)
        rank = ranks(valid)
        limit = pack(taken)
        begin = pack(column(start))
        blocks = pack(index)
        if is_first:
            keep, at_place = (valid > 0.5) & (rank < limit), begin + rank
        else:
            keep, at_place = (valid > 0.5) & (rank >= limit), begin + rank - limit
        at_place = jnp.where(keep, at_place, -1.0)
        table = jnp.zeros((8, 128), jnp.float32)
        for m in range(4):
            hit = ones(at_place[m : m + 1, :].astype(jnp.int32) == place)
            table = jnp.where(row == m, dot_t(blocks, hit), table)
        out.append(table)
    return jnp.clip(jnp.concatenate(out, axis=0).astype(jnp.int32), 0, blocks_held - 1)


def second_tables(first, second, one_first, one_second, two_first, two_second, y, z):
    r, k = grid(8, 16)
    row, lane = grid(8, 128)
    spot = lane.astype(jnp.float32)
    last = STAY + 3 * CAP_ONE - 1
    out = []
    for count, one, two, rows, me, far in (
        (first, one_first, two_first, ones((k == y * 4 + r) & (r < 4)), y, lambda i: i * 4 + z),
        (second, one_second, two_second, ones((k == r * 4 + z) & (r < 4)), z, lambda i: y * 4 + i),
    ):
        count, one, two = dot(rows, count), dot(rows, one), dot(rows, two)
        table = jnp.zeros((8, 128), jnp.float32)
        for i in range(4):
            pick = lane == far(i)
            n = jnp.sum(jnp.where(pick, count, 0.0), axis=1, keepdims=True)
            begin = jnp.sum(jnp.where(pick, one, 0.0), axis=1, keepdims=True)
            shift = jnp.sum(jnp.where(pick, two, 0.0), axis=1, keepdims=True)
            base = part_of((me - i + 4) % 4, CAP_ONE)
            inside = (spot >= shift) & (spot < shift + n)
            table = jnp.where(inside, begin + spot - shift + jnp.full((8, 128), base).astype(jnp.float32), table)
        out.append(table)
    return jnp.clip(jnp.concatenate(out, axis=0).astype(jnp.int32), 0, last)


def part_of(distance, cap):
    return jnp.where(distance == 0, 0, STAY + (distance - 1) * cap)


def final_table(slots, first, two_first, two_second, y, z):
    valid = ones(slots < 255.5)
    rank = ranks(valid)
    r, k = grid(8, 16)
    row, lane = grid(8, 128)
    a, b = grid(128, 128)
    spread = ones((a % 4 == b // 32) & (a < 16))

    def own(table):
        picked = dot(ones(k == y * 4 + z), table)
        return dot(jnp.where((lane // 4 == row) & (lane < 16), picked, 0.0), spread)

    limit, shift_first, shift_second = own(first), own(two_first), own(two_second)
    total = STAY + 3 * CAP_TWO
    base_first = part_of((z - lane // 32 + 4) % 4, CAP_TWO).astype(jnp.float32)
    base_second = (part_of((y - row + 8) % 4, CAP_TWO) + total).astype(jnp.float32)
    spot = jnp.where(rank < limit, base_first + shift_first + rank, base_second + shift_second + rank - limit)
    spot = jnp.clip(spot, 0.0, float(2 * total - 1))
    high = jnp.floor(spot / 16.0)
    low = spot - high * 16.0
    place, _ = grid(256, 128)
    found = jnp.zeros((8, 256), jnp.float32)
    for m in range(4):
        hit = ones(slots[m : m + 1, :].astype(jnp.int32) == place)
        found = found + dot_t(jnp.where(row == m, high, 0.0), hit) * 16.0 + dot_t(jnp.where(row == m, low, 0.0), hit)
    return jnp.clip(jnp.sum(found, axis=0, keepdims=True).astype(jnp.int32), 0, 2 * total - 1)


def step_kernel(
    recv_h, sidx_h, holder, lengths, hidden_h, gain_h, pool_h, wq_h, wkv_h, w_h,
    cache, out, q_o, kv_o, over_o,
    recv_v, sidx_v, pool, masks, one_v, two_v, inv_v, one_s, two_s, inv_s, stage_one, mid, stage_two, fin, held,
    wq, wkv, w, hidden, gain, hpeer, kvsend, kvpeer, normed, att, part, paired, land, land_hidden, mate_in,
    send, recv, side_send, side_recv, mask_send, mask_recv, tail_send, tail_recv, local,
):
    y, z, tp = place()
    rep = lax.axis_index("rep")
    count = lax.axis_size("tp")
    copies = [
        pltpu.make_async_copy(src, dst, local.at[i])
        for i, (src, dst) in enumerate(
            ((recv_h, recv_v), (sidx_h, sidx_v), (hidden_h, hidden), (pool_h, pool), (gain_h, gain), (wkv_h, wkv), (wq_h, wq), (w_h, w))
        )
    ]
    recv_in, sidx_in, hidden_in, pool_in, gain_in, wkv_in, wq_in, w_in = copies
    for copy in copies[:5]:
        copy.start()

    barrier = pltpu.get_barrier_semaphore()
    for d in FAR:
        for device in (at((y + d) % 4, z), at(y, (z + d) % 4)):
            pl.semaphore_signal(barrier, inc=1, device_id=device, device_id_type=MESH)
    others = announce(barrier)

    recv_in.wait()
    row, _ = grid(8, 128)
    slots = jnp.where(row < 4, pack_y(widen(ring_order(recv_v[...]))), 256.0)
    masks[z, y] = ones(slots < 255.5)
    pl.semaphore_wait(barrier, 6 + others)

    hops = []
    for d in FAR:
        copy = remote(masks.at[z, y], masks.at[z, y], mask_send, mask_recv, d - 1, at((y + d) % 4, z))
        copy.start()
        hops.append(copy)
    for copy in hops:
        copy.wait_recv()
    for d in FAR:
        copy = remote(masks.at[z], masks.at[z], mask_send, mask_recv, 3 + d - 1, at(y, (z + d) % 4))
        copy.start()
        hops.append(copy)
    for copy in hops[3:]:
        copy.wait_recv()
    for copy in hops:
        copy.wait_send()

    peer = {"rep": 1 - rep}
    hidden_in.wait()
    share = hidden.shape[1] // count
    eighth = pl.ds(pl.multiple_of(tp * share, share), share)
    to_peer = remote(hidden.at[:, eighth], hpeer.at[:, eighth], side_send, side_recv, 0, peer)
    to_peer.start()
    ahead = send_hidden(hidden, land_hidden, tail_send, tail_recv)

    first, second, over = route(masks, y, z)
    one_first, one_second, two_first, two_second = offsets(first, second)
    sidx_in.wait()
    index = widen(ring_order(sidx_v[...]))
    table = first_tables(masks, index, first, one_first, one_second, y, z, pool.shape[0])
    row, _ = grid(16, 128)
    one_v[...] = jnp.where(row == 4, jnp.broadcast_to(over, (16, 128)).astype(jnp.int32), table)
    one_in = pltpu.make_async_copy(one_v, one_s, local.at[8])
    one_in.start()
    pool_in.wait()
    one_in.wait()
    over_o[0] = one_s[4, 0]

    def pack(dst, begin, count, src, table, line):
        unroll = 8

        def body(i, _):
            for u in range(unroll):
                p = i * unroll + u
                dst[begin + p] = src[table[line, p]]
            return 0

        lax.fori_loop(0, count // unroll, body, 0)
        for p in range(count // unroll * unroll, count):
            dst[begin + p] = src[table[line, p]]

    stay_one = STAY + 3 * CAP_ONE
    stay_two = STAY + 3 * CAP_TWO
    started = []
    for d in FAR:
        for way, line, device in ((0, (y + d) % 4, at((y + d) % 4, z)), (1, 8 + (z + d) % 4, at(y, (z + d) % 4))):
            begin = (way * 3 + d - 1) * CAP_ONE
            pack(stage_one, begin, CAP_ONE, pool, one_s, line)
            copy = remote(
                stage_one.at[pl.ds(begin, CAP_ONE)],
                mid.at[way, pl.ds(STAY + (d - 1) * CAP_ONE, CAP_ONE)],
                send, recv, way * 3 + d - 1, device,
            )
            copy.start()
            started.append(copy)
    wkv_in.start()
    wq_in.start()
    w_in.start()
    to_peer.wait_recv()
    shared = []
    for k in range(1, count):
        copy = remote(
            hpeer.at[:, eighth], hpeer.at[:, eighth], side_send, side_recv, 1 + k, {"tp": (tp + k) % count}
        )
        copy.start()
        shared.append(copy)
    pack(mid.at[0], 0, STAY, pool, one_s, y)
    pack(mid.at[1], 0, STAY, pool, one_s, 8 + z)

    two_v[...] = second_tables(first, second, one_first, one_second, two_first, two_second, y, z)
    two_in = pltpu.make_async_copy(two_v, two_s, local.at[9])
    two_in.start()
    inv_v[...] = final_table(slots, first, two_first, two_second, y, z)
    inv_in = pltpu.make_async_copy(inv_v, inv_s, local.at[10])
    inv_in.start()

    gain_in.wait()
    for copy in shared:
        copy.wait_recv()
    width = hidden.shape[1]
    step = 1024
    rows = hidden.shape[0]

    def scale_of(ref):
        total = jnp.zeros((rows, 1), jnp.float32)
        for i in range(width // step):
            part = ref[:, i * step : (i + 1) * step].astype(jnp.float32)
            total = total + jnp.sum(part * part, axis=1, keepdims=True)
        return lax.rsqrt(total / width + 1e-05)

    own_scale, peer_scale = scale_of(hidden), scale_of(hpeer)
    for i in range(width // step):
        cut = slice(i * step, (i + 1) * step)
        g = gain[:, cut]
        normed[0:rows, cut] = (hidden[:, cut].astype(jnp.float32) * own_scale * g).astype(jnp.bfloat16)
        normed[rows : 2 * rows, cut] = (hpeer[:, cut].astype(jnp.float32) * peer_scale * g).astype(jnp.bfloat16)

    def product(count, weight):
        def body(i, total):
            cut = pl.ds(pl.multiple_of(i * step, step), step)
            return total + jnp.dot(normed[0:count, cut], weight[cut, :], preferred_element_type=jnp.float32)

        return lax.fori_loop(0, width // step, body, jnp.zeros((count, weight.shape[1]), jnp.float32))

    wkv_in.wait()
    both = product(2 * rows, wkv).astype(jnp.bfloat16)
    kvsend[...] = both[rows : 2 * rows]
    back = remote(kvsend, kvpeer, side_send, side_recv, 1, peer)
    back.start()
    wq_in.wait()
    query = product(rows, wq).astype(jnp.bfloat16).astype(jnp.float32)
    q_o[...] = jnp.zeros_like(q_o)
    for h in range(query.shape[1] // HD):
        q_o[:, h, :] = query[:, h * HD : (h + 1) * HD]
    back.wait_recv()
    mine = jnp.where(holder[0] == rep, jnp.float32(1), jnp.float32(0))
    own = both[0:rows].astype(jnp.float32)
    other = kvpeer[...].astype(jnp.float32)
    kv_o[...] = jnp.where(jnp.full(own.shape, mine) > 0.5, own, other).astype(jnp.bfloat16)

    two_in.wait()
    for copy in started:
        copy.wait_recv()
    relays = []
    for d in FAR:
        for way, line, device in ((0, (z + d) % 4, at(y, (z + d) % 4)), (1, 8 + (y + d) % 4, at((y + d) % 4, z))):
            begin = (way * 3 + d - 1) * CAP_TWO
            pack(stage_two, begin, CAP_TWO, mid.at[way], two_s, line)
            copy = remote(
                stage_two.at[pl.ds(begin, CAP_TWO)],
                fin.at[pl.ds(way * stay_two + STAY + (d - 1) * CAP_TWO, CAP_TWO)],
                send, recv, 6 + way * 3 + d - 1, device,
            )
            copy.start()
            relays.append(copy)
    for way, line in ((0, z), (1, 8 + y)):
        pack(fin, way * stay_two, STAY, mid.at[way], two_s, line)
    inv_in.wait()
    w_in.wait()
    for copy in [to_peer, back, *shared, *started]:
        copy.wait_send()
    for copy in relays:
        copy.wait_recv()

    per = held.shape[0] // rows
    extra = 2 * stay_two
    for b in range(rows):
        length = lengths[b]
        fin[extra + b] = renewed(fin[inv_s[0, b * per + length // BLK]], length, kv_o[b : b + 1, :])

    def order(b, _):
        changed = lengths[b] // BLK
        for i in range(per):
            source = jnp.where(changed == i, extra + b, inv_s[0, b * per + i])
            held[b * per + i] = fin[source]
        return 0

    lax.fori_loop(0, rows, order, 0)
    store = pltpu.make_async_copy(held, cache, local.at[11])
    store.start()
    for b in range(rows):
        attention(held, q_o, lengths, att, b)
    project(att, w, part)
    summed(part, out, paired, land, land_hidden, mate_in, tail_send, tail_recv, ahead)
    for copy in relays:
        copy.wait_send()
    store.wait()


def hand_kernel(source, cache, held, read, written):
    count = read.shape[0]
    per = source.shape[0] // count
    reads, writes = [], []
    for i in range(count):
        part = pl.ds(i * per, per)
        reads.append(pltpu.make_async_copy(source.at[part], held.at[part], read.at[i]))
        writes.append(pltpu.make_async_copy(held.at[part], cache.at[part], written.at[i]))
    for copy in reads:
        copy.start()
    for one, other in zip(reads, writes, strict=True):
        one.wait()
        other.start()
    for copy in writes:
        copy.wait()


def whole_kernel(sidx, pool_h, land, pool, stage, send, recv, local):
    y, z, _ = place()
    pool_in = pltpu.make_async_copy(pool_h, pool, local.at[0])
    pool_in.start()
    pairs = [(dy, dz) for dy in range(4) for dz in range(4) if dy or dz]
    barrier = pltpu.get_barrier_semaphore()
    for dy, dz in pairs:
        pl.semaphore_signal(barrier, inc=1, device_id=at((y + dy) % 4, (z + dz) % 4), device_id_type=MESH)
    pl.semaphore_wait(barrier, len(pairs))
    pool_in.wait()
    me = group(y, z)
    copies = []
    for dy, dz in [(0, 0), *pairs]:
        g = group((y + dy) % 4, (z + dz) % 4)
        k = dy * 4 + dz

        def body(c, _):
            stage[k, c] = pool[sidx[g, c]]
            return 0

        lax.fori_loop(0, stage.shape[1], body, 0)
        if k:
            copy = remote(stage.at[k], land.at[me], send, recv, k - 1, at((y + dy) % 4, (z + dz) % 4))
        else:
            copy = pltpu.make_async_copy(stage.at[0], land.at[me], local.at[1])
        copy.start()
        copies.append(copy)
    for copy in copies:
        copy.wait()


def attention(held, q, lengths, att, b):
    per = held.shape[0] // q.shape[0]
    keys = held[b * per : (b + 1) * per, :, 0:HD].reshape(CTX, HD)
    values = held[b * per : (b + 1) * per, :, HD : 2 * HD].reshape(CTX, HD)
    scores = lax.dot_general(
        q[b].astype(jnp.bfloat16), keys, (((1,), (1,)), ((), ())), preferred_element_type=jnp.float32
    ) * HD ** (-0.5)
    valid = lax.broadcasted_iota(jnp.int32, scores.shape, 1) <= lengths[b]
    expo = jnp.where(valid, jnp.exp(jnp.where(valid, scores, 0.0)), 0.0)
    weights = (expo / jnp.sum(expo, axis=1, keepdims=True)).astype(jnp.bfloat16)
    att[b] = jnp.dot(weights, values, preferred_element_type=jnp.float32)


def project(att, w, part):
    heads = w.shape[0] // HD
    attended = jnp.concatenate([att[:, h, :] for h in range(heads)], axis=1).astype(jnp.bfloat16)
    step = part.shape[3]
    for t in range(part.shape[0] * part.shape[1]):
        chunk = jnp.dot(attended, w[:, t * step : (t + 1) * step], preferred_element_type=jnp.float32)
        part[t % 2, t // 2] = chunk.astype(jnp.bfloat16)


def renewed(block, length, fresh):
    row, _ = grid(*block.shape)
    fresh = jnp.broadcast_to(fresh.astype(jnp.float32), block.shape)
    return jnp.where(row == length % BLK, fresh, block.astype(jnp.float32)).astype(jnp.bfloat16)


def attend_kernel(inv, lengths, land, q, kv, w_h, cache, part, held, w, att, ready, stored, loaded):
    requests = q.shape[0]
    per = held.shape[0] // requests

    def span(b):
        return pl.ds(b * per, per)

    def fetch(b, _):
        for u in range(per):
            j = b * per + u
            pltpu.make_async_copy(land.at[inv[j]], held.at[j], ready.at[b]).start()
        return 0

    lax.fori_loop(0, requests, fetch, 0)
    w_in = pltpu.make_async_copy(w_h, w, loaded.at[0])
    w_in.start()
    stores = []
    for b in range(requests):
        pltpu.make_async_copy(land.at[pl.ds(0, per)], held.at[span(b)], ready.at[b]).wait()
        length = lengths[b]
        j = b * per + length // BLK
        held[j] = renewed(held[j], length, kv[b : b + 1, :])
        store = pltpu.make_async_copy(held.at[span(b)], cache.at[span(b)], stored.at[b])
        store.start()
        stores.append(store)
        attention(held, q, lengths, att, b)
    w_in.wait()
    project(att, w, part)
    for store in stores:
        store.wait()


def summed(part, out, paired, land, land_hidden, mate_in, send, recv, arriving):
    tp = lax.axis_index("tp")
    section = lax.axis_index("section")
    chips = part.shape[1]
    step = part.shape[3]
    core, chip = tp % 2, tp // 2
    mate = {"tp": chip * 2 + 1 - core}
    after = (section + 1) % lax.axis_size("section")

    def cut(t):
        return pl.ds(pl.multiple_of(t * step, step), step)

    def along(d):
        return ((chip + d) % chips) * 2 + core

    swap = remote(part.at[1 - core], mate_in, send, recv, 0, mate)
    swap.start()
    swap.wait_recv()
    sums = []
    for d in (*FAR, 0):
        x = (chip + d) % chips
        both = part[core, x].astype(jnp.float32) + mate_in[x].astype(jnp.float32)
        paired[d] = both.astype(jnp.bfloat16)
        copy = remote(paired.at[d], land.at[d], send, recv, 2 + d, {"section": after, "tp": along(d)})
        copy.start()
        sums.append(copy)
    arriving.wait_recv()
    total = land_hidden[...].astype(jnp.float32)
    for copy, d in zip(sums, (*FAR, 0), strict=True):
        copy.wait_recv()
        total = total + land[d].astype(jnp.float32)
    out[:, cut(tp)] = total.astype(jnp.bfloat16)

    spread = []
    for d in FAR:
        copy = remote(out.at[:, cut(tp)], out.at[:, cut(tp)], send, recv, 6 + d, {"tp": along(d)})
        copy.start()
        spread.append(copy)
    passed = [remote(out.at[:, cut(tp)], out.at[:, cut(tp)], send, recv, 10, mate)]
    passed[0].start()
    for copy, d in zip(spread, FAR, strict=True):
        copy.wait_recv()
        t = along(chips - d)
        onward = remote(out.at[:, cut(t)], out.at[:, cut(t)], send, recv, 10 + d, mate)
        onward.start()
        passed.append(onward)
    for copy in passed:
        copy.wait_recv()
    for copy in [swap, arriving, *sums, *spread, *passed]:
        copy.wait_send()


def announce(barrier):
    tp = lax.axis_index("tp")
    section = lax.axis_index("section")
    sections = lax.axis_size("section")
    count = lax.axis_size("tp")
    before = (section + sections - 1) % sections
    for d in range(count // 2):
        pl.semaphore_signal(
            barrier, inc=1, device_id={"section": before, "tp": (tp + 2 * d) % count}, device_id_type=MESH
        )
    for k in range(1, count):
        pl.semaphore_signal(barrier, inc=1, device_id={"tp": (tp + k) % count}, device_id_type=MESH)
    return count // 2 + count - 1


def send_hidden(hidden, land_hidden, send, recv):
    tp = lax.axis_index("tp")
    step = land_hidden.shape[1]
    after = (lax.axis_index("section") + 1) % lax.axis_size("section")
    own = pl.ds(pl.multiple_of(tp * step, step), step)
    ahead = remote(hidden.at[:, own], land_hidden, send, recv, 1, {"section": after})
    ahead.start()
    return ahead


def finish_kernel(part, hidden, out, paired, land, land_hidden, mate_in, send, recv):
    barrier = pltpu.get_barrier_semaphore()
    pl.semaphore_wait(barrier, announce(barrier))
    ahead = send_hidden(hidden, land_hidden, send, recv)
    summed(part, out, paired, land, land_hidden, mate_in, send, recv, ahead)


def shards(
    hidden, gain, w_query, w_keyval, w_out, old_pool, send_index, recv_slot, holder, lengths
):
    state = hidden[0, 0]
    requests, width = state.shape
    pool_blocks, blk, lanes = old_pool.shape
    groups, cap = send_index.shape[1:]
    blocks = requests * CTX // blk
    heads = w_query.shape[2] // HD
    vmem = pl.BlockSpec(memory_space=pltpu.VMEM)
    smem = pl.BlockSpec(memory_space=pltpu.SMEM)
    hbm = pl.BlockSpec(memory_space=pl.ANY)

    tp = lax.axis_size("tp")
    chips = tp // 2
    chunk = width // tp
    dma = pltpu.SemaphoreType.DMA
    blocks_of = jax.ShapeDtypeStruct((blocks, blk, lanes), jnp.bfloat16)
    rows_of = jax.ShapeDtypeStruct((requests, width), jnp.bfloat16)
    tail = [
        pltpu.VMEM((chips, requests, chunk), jnp.bfloat16),
        pltpu.VMEM((chips, requests, chunk), jnp.bfloat16),
        pltpu.VMEM((requests, chunk), jnp.bfloat16),
        pltpu.VMEM((chips, requests, chunk), jnp.bfloat16),
    ]

    def params(limit, **more):
        return pltpu.CompilerParams(vmem_limit_bytes=limit * MIB, **more)

    quick_cache, quick_passed, query, keyval, over = pl.pallas_call(
        step_kernel,
        name="step",
        out_shape=(
            blocks_of,
            rows_of,
            jax.ShapeDtypeStruct((requests, 8, HD), jnp.float32),
            jax.ShapeDtypeStruct((requests, lanes), jnp.bfloat16),
            jax.ShapeDtypeStruct((1,), jnp.int32),
        ),
        in_specs=[hbm, hbm, smem, smem, hbm, hbm, hbm, hbm, hbm, hbm],
        out_specs=(hbm, vmem, vmem, vmem, smem),
        scratch_shapes=[
            pltpu.VMEM((groups, cap), jnp.int32),
            pltpu.VMEM((groups, cap), jnp.int32),
            pltpu.VMEM((pool_blocks, blk, lanes), jnp.bfloat16),
            pltpu.VMEM((4, 4, 8, 128), jnp.float32),
            pltpu.VMEM((16, 128), jnp.int32),
            pltpu.VMEM((16, 128), jnp.int32),
            pltpu.VMEM((1, blocks), jnp.int32),
            pltpu.SMEM((16, 128), jnp.int32),
            pltpu.SMEM((16, 128), jnp.int32),
            pltpu.SMEM((1, blocks), jnp.int32),
            pltpu.VMEM((6 * CAP_ONE, blk, lanes), jnp.bfloat16),
            pltpu.VMEM((2, STAY + 3 * CAP_ONE, blk, lanes), jnp.bfloat16),
            pltpu.VMEM((6 * CAP_TWO, blk, lanes), jnp.bfloat16),
            pltpu.VMEM((2 * (STAY + 3 * CAP_TWO) + requests, blk, lanes), jnp.bfloat16),
            pltpu.VMEM((blocks, blk, lanes), jnp.bfloat16),
            pltpu.VMEM(w_query.shape[1:], jnp.bfloat16),
            pltpu.VMEM(w_keyval.shape[2:], jnp.bfloat16),
            pltpu.VMEM(w_out.shape[1:], jnp.bfloat16),
            pltpu.VMEM((requests, width), jnp.bfloat16),
            pltpu.VMEM((1, width), jnp.float32),
            pltpu.VMEM((requests, width), jnp.bfloat16),
            pltpu.VMEM((requests, lanes), jnp.bfloat16),
            pltpu.VMEM((requests, lanes), jnp.bfloat16),
            pltpu.VMEM((2 * requests, width), jnp.bfloat16),
            pltpu.VMEM((requests, 8, HD), jnp.float32),
            pltpu.VMEM((2, chips, requests, chunk), jnp.bfloat16),
            *tail,
            dma((12,)),
            dma((12,)),
            dma((tp + 1,)),
            dma((tp + 1,)),
            dma((6,)),
            dma((6,)),
            dma((14,)),
            dma((14,)),
            dma((12,)),
        ],
        compiler_params=params(62, collective_id=0, has_side_effects=True),
    )(
        recv_slot[0], send_index[0], holder, lengths[0, 0], state, gain, old_pool, w_query[0], w_keyval[0, 0], w_out[0]
    )

    def quick():
        handed = pl.pallas_call(
            hand_kernel,
            name="hand",
            out_shape=blocks_of,
            in_specs=[hbm],
            out_specs=hbm,
            scratch_shapes=[pltpu.VMEM((blocks, blk, lanes), jnp.bfloat16), dma((16,)), dma((16,))],
            compiler_params=params(60),
        )(quick_cache)
        return handed, quick_passed

    def whole():
        arrived = pl.pallas_call(
            whole_kernel,
            name="whole",
            out_shape=jax.ShapeDtypeStruct((groups, cap, blk, lanes), jnp.bfloat16),
            in_specs=[smem, hbm],
            out_specs=hbm,
            scratch_shapes=[
                pltpu.VMEM((pool_blocks, blk, lanes), jnp.bfloat16),
                pltpu.VMEM((groups, cap, blk, lanes), jnp.bfloat16),
                dma((15,)),
                dma((15,)),
                dma((2,)),
            ],
            compiler_params=params(60, collective_id=2, has_side_effects=True),
        )(send_index[0], old_pool)
        hit = recv_slot[0].reshape(1, -1) == jnp.arange(blocks, dtype=jnp.int32)[:, None]
        inverse = jnp.sum(jnp.where(hit, jnp.arange(groups * cap, dtype=jnp.int32)[None, :], 0), axis=1)
        cache, part = pl.pallas_call(
            attend_kernel,
            name="attend",
            out_shape=(blocks_of, jax.ShapeDtypeStruct((2, chips, requests, chunk), jnp.bfloat16)),
            in_specs=[smem, smem, hbm, vmem, vmem, hbm],
            out_specs=(hbm, vmem),
            scratch_shapes=[
                pltpu.VMEM((blocks, blk, lanes), jnp.bfloat16),
                pltpu.VMEM(w_out.shape[1:], jnp.bfloat16),
                pltpu.VMEM((requests, 8, HD), jnp.float32),
                dma((requests,)),
                dma((requests,)),
                dma((1,)),
            ],
            compiler_params=params(60),
        )(inverse, lengths[0, 0], arrived.reshape(groups * cap, blk, lanes), query, keyval, w_out[0])
        passed = pl.pallas_call(
            finish_kernel,
            name="finish",
            out_shape=rows_of,
            in_specs=[vmem, vmem],
            out_specs=vmem,
            scratch_shapes=[*tail, dma((14,)), dma((14,))],
            compiler_params=params(57, collective_id=1, has_side_effects=True),
        )(part, state)
        return cache, passed

    cache, passed = lax.cond(over[0] > 0, whole, quick)
    return passed[None, None], cache.reshape(1, 1, requests, CTX, lanes)


def solution(mesh):
    in_specs = (
        P("rep", "section", None, None),
        P("section", None),
        P("section", None, "tp"),
        P("rep", "section", None, "tp"),
        P("section", "tp", None),
        P(("rep", "section"), None, "tp"),
        P(("rep", "section"), None, None),
        P(("rep", "section"), None, None),
        P("section"),
        P("rep", "section", None),
    )
    out_specs = (P("rep", "section", None, None), P("rep", "section", None, None, "tp"))
    return jax.shard_map(shards, mesh=mesh, in_specs=in_specs, out_specs=out_specs, check_vma=False)
```

```python
import functools

import jax
import jax.numpy as jnp
from jax import lax
from jax.experimental import pallas as pl
from jax.experimental.pallas import tpu as pltpu
from jax.sharding import PartitionSpec as P

HD = 128
CTX = 512
BLK = 32
MESH = pl.DeviceIdType.MESH
MIB = 2**20
FAR = (1, 3, 2)
LONG = (2, 1, 3, 0)
OTHERS = sorted(
    ((dy, dz) for dy in range(4) for dz in range(4) if dy or dz),
    key=lambda d: -(min(d[0], 4 - d[0]) + min(d[1], 4 - d[1])),
)
CAP_ONE = 41
CAP_TWO = 41
STAY = 128
BALANCE = (0.016, 0.01, 0.006)


def place():
    rep, section = lax.axis_index("rep"), lax.axis_index("section")
    return (section // 4) * 2 + rep, section % 4, lax.axis_index("tp")


def at(y, z):
    return {"rep": y % 2, "section": (y // 2) * 4 + z}


def group(y, z):
    return (y % 2) * 8 + (y // 2) * 4 + z


def remote(src, dst, send, recv, k, device):
    return pltpu.make_async_remote_copy(
        src_ref=src,
        dst_ref=dst,
        send_sem=send.at[k],
        recv_sem=recv.at[k],
        device_id=device,
        device_id_type=MESH,
    )


def dot(a, b):
    return jnp.dot(a.astype(jnp.bfloat16), b.astype(jnp.bfloat16), preferred_element_type=jnp.float32)


def dot_t(a, b):
    return lax.dot_general(
        a.astype(jnp.bfloat16), b.astype(jnp.bfloat16), (((1,), (1,)), ((), ())), preferred_element_type=jnp.float32
    )


def grid(rows, columns):
    return (
        lax.broadcasted_iota(jnp.int32, (rows, columns), 0),
        lax.broadcasted_iota(jnp.int32, (rows, columns), 1),
    )


def ones(condition):
    return jnp.where(condition, 1.0, 0.0).astype(jnp.float32)


def ring_order(table):
    return jnp.concatenate([table[0:4], table[8:12], table[4:8], table[12:16]], axis=0).astype(jnp.float32)


def widen(table):
    k, lane = grid(32, 128)
    return dot(table, ones(k == lane % 32))


def pack_y(table):
    row, lane = grid(16, 128)
    r, k = grid(8, 16)
    return dot(ones(k // 4 == r), jnp.where(lane // 32 == row % 4, table, 0.0))


def pack_z(table):
    row, lane = grid(16, 128)
    r, k = grid(8, 16)
    return dot(ones((k % 4 == r) & (r < 4)), jnp.where(lane // 32 == row // 4, table, 0.0))


def ranks(valid):
    k, lane = grid(128, 128)
    return dot(valid, ones((k < lane) & (k // 32 == lane // 32)))


def route(masks, y, z):
    flat = masks[...].reshape(128, 128)
    k, lane = grid(128, 128)
    per = dot(flat, ones((k // 32 == lane % 4) & (lane < 16)))
    per = jnp.where((lane // 4 == k % 8) & (lane < 16), per, 0.0)
    g, k = grid(16, 128)
    counts = dot(ones(k // 8 == (g % 4) * 4 + g // 4), per)

    g, h = grid(16, 128)
    inside = h < 16
    off_y = ones((g // 4 != h // 4) & inside)
    off_z = ones((g % 4 != h % 4) & inside)
    a, b = grid(16, 16)
    same_y, same_z = ones(a // 4 == b // 4), ones(a % 4 == b % 4)
    a, b = grid(128, 128)
    both = (a < 16) & (b < 16)
    along_y, along_z = ones((a // 4 == b // 4) & both), ones((a % 4 == b % 4) & both)

    def loads(first, second):
        return (
            dot(same_y, first) * off_y,
            dot(same_z, second) * off_z,
            dot(first, along_z) * off_z,
            dot(second, along_y) * off_y,
        )

    share = jnp.full((16, 128), 0.5, jnp.float32)
    for pace in BALANCE:
        a1, b1, a2, b2 = loads(counts * share, counts - counts * share)
        share = jnp.clip(share + pace * (jnp.maximum(b1, b2) - jnp.maximum(a1, a2)), 0.0, 1.0)
    share = jnp.where(g == h, 1.0, share)
    first = jnp.floor(counts * share + 0.5)
    second = counts - first
    a1, b1, a2, b2 = loads(first, second)
    over = jnp.maximum(jnp.maximum(a1, b1) - CAP_ONE, jnp.maximum(a2, b2) - CAP_TWO)
    return first, second, jnp.max(over, keepdims=True)


def offsets(first, second):
    a, b = grid(16, 16)
    one_first = dot(ones((a // 4 == b // 4) & (b % 4 < a % 4)), first)
    one_second = dot(ones((a % 4 == b % 4) & (b // 4 < a // 4)), second)
    a, b = grid(128, 128)
    both = (a < 16) & (b < 16)
    two_first = dot(first, ones((a % 4 == b % 4) & (a // 4 < b // 4) & both))
    two_second = dot(second, ones((a // 4 == b // 4) & (a % 4 < b % 4) & both))
    return one_first, one_second, two_first, two_second


def first_tables(masks, index, first, one_first, one_second, y, z, blocks_held):
    flat = masks[...].reshape(128, 128)
    g, k = grid(16, 128)
    mine = dot(ones(k == ((g % 4) * 4 + g // 4) * 8 + y), flat)
    k, lane = grid(128, 128)
    mine = dot(mine, ones(k == z * 32 + lane % 32))
    g, h = grid(16, 128)

    def column(table):
        picked = jnp.sum(jnp.where(h == y * 4 + z, table, 0.0), axis=1, keepdims=True)
        return jnp.broadcast_to(picked, (16, 128))

    taken = column(first)
    place, lane = grid(128, 128)
    row, _ = grid(8, 128)
    out = []
    for pack, start, is_first in ((pack_y, one_first, True), (pack_z, one_second, False)):
        valid = pack(mine)
        rank = ranks(valid)
        limit = pack(taken)
        begin = pack(column(start))
        blocks = pack(index)
        if is_first:
            keep, at_place = (valid > 0.5) & (rank < limit), begin + rank
        else:
            keep, at_place = (valid > 0.5) & (rank >= limit), begin + rank - limit
        at_place = jnp.where(keep, at_place, -1.0)
        table = jnp.zeros((8, 128), jnp.float32)
        for m in range(4):
            hit = ones(at_place[m : m + 1, :].astype(jnp.int32) == place)
            table = jnp.where(row == m, dot_t(blocks, hit), table)
        out.append(table)
    return jnp.clip(jnp.concatenate(out, axis=0).astype(jnp.int32), 0, blocks_held - 1)


def second_tables(first, second, one_first, one_second, two_first, two_second, y, z):
    r, k = grid(8, 16)
    row, lane = grid(8, 128)
    spot = lane.astype(jnp.float32)
    last = STAY + 3 * CAP_ONE - 1
    out = []
    for count, one, two, rows, me, far in (
        (first, one_first, two_first, ones((k == y * 4 + r) & (r < 4)), y, lambda i: i * 4 + z),
        (second, one_second, two_second, ones((k == r * 4 + z) & (r < 4)), z, lambda i: y * 4 + i),
    ):
        count, one, two = dot(rows, count), dot(rows, one), dot(rows, two)
        table = jnp.zeros((8, 128), jnp.float32)
        for i in range(4):
            pick = lane == far(i)
            n = jnp.sum(jnp.where(pick, count, 0.0), axis=1, keepdims=True)
            begin = jnp.sum(jnp.where(pick, one, 0.0), axis=1, keepdims=True)
            shift = jnp.sum(jnp.where(pick, two, 0.0), axis=1, keepdims=True)
            base = part_of((me - i + 4) % 4, CAP_ONE)
            inside = (spot >= shift) & (spot < shift + n)
            table = jnp.where(inside, begin + spot - shift + jnp.full((8, 128), base).astype(jnp.float32), table)
        out.append(table)
    return jnp.clip(jnp.concatenate(out, axis=0).astype(jnp.int32), 0, last)


def part_of(distance, cap):
    return jnp.where(distance == 0, 0, STAY + (distance - 1) * cap)


def final_table(slots, first, two_first, two_second, y, z):
    valid = ones(slots < 255.5)
    rank = ranks(valid)
    r, k = grid(8, 16)
    row, lane = grid(8, 128)
    a, b = grid(128, 128)
    spread = ones((a % 4 == b // 32) & (a < 16))

    def own(table):
        picked = dot(ones(k == y * 4 + z), table)
        return dot(jnp.where((lane // 4 == row) & (lane < 16), picked, 0.0), spread)

    limit, shift_first, shift_second = own(first), own(two_first), own(two_second)
    total = STAY + 3 * CAP_TWO
    base_first = part_of((z - lane // 32 + 4) % 4, CAP_TWO).astype(jnp.float32)
    base_second = (part_of((y - row + 8) % 4, CAP_TWO) + total).astype(jnp.float32)
    spot = jnp.where(rank < limit, base_first + shift_first + rank, base_second + shift_second + rank - limit)
    spot = jnp.clip(spot, 0.0, float(2 * total - 1))
    high = jnp.floor(spot / 16.0)
    low = spot - high * 16.0
    place, _ = grid(256, 128)
    found = jnp.zeros((8, 256), jnp.float32)
    for m in range(4):
        hit = ones(slots[m : m + 1, :].astype(jnp.int32) == place)
        found = found + dot_t(jnp.where(row == m, high, 0.0), hit) * 16.0 + dot_t(jnp.where(row == m, low, 0.0), hit)
    return jnp.clip(jnp.sum(found, axis=0, keepdims=True).astype(jnp.int32), 0, 2 * total - 1)


def step_kernel(
    recv_h, sidx_h, holder, lengths, hidden_h, gain_h, pool_h, wq_h, wkv_h, w_h,
    cache, out, q_o, kv_o, over_o,
    recv_v, sidx_v, pool, masks, one_v, two_v, inv_v, one_s, two_s, inv_s, stage_one, mid, stage_two, fin, changed_blocks, held,
    wq, wkv, w, hidden, gain, hpeer, kvsend, kvpeer, normed, att, give, kept, paired, land, land_hidden, mate_in,
    send, recv, side_send, side_recv, mask_send, mask_recv, tail_send, tail_recv, local,
):
    y, z, tp = place()
    rep = lax.axis_index("rep")
    count = lax.axis_size("tp")
    copies = [
        pltpu.make_async_copy(src, dst, local.at[i])
        for i, (src, dst) in enumerate(
            ((recv_h, recv_v), (sidx_h, sidx_v), (hidden_h, hidden), (pool_h, pool), (gain_h, gain), (wkv_h, wkv), (wq_h, wq), (w_h, w))
        )
    ]
    recv_in, sidx_in, hidden_in, pool_in, gain_in, wkv_in, wq_in, w_in = copies
    for copy in copies[:5]:
        copy.start()

    barrier = pltpu.get_barrier_semaphore()
    others = announce(barrier)
    for dy, dz in OTHERS:
        device = at((y + dy) % 4, (z + dz) % 4)
        pl.semaphore_signal(barrier, inc=1, device_id=device, device_id_type=MESH)

    recv_in.wait()
    row, _ = grid(8, 128)
    slots = jnp.where(row < 4, pack_y(widen(ring_order(recv_v[...]))), 256.0)
    masks[z, y] = ones(slots < 255.5)
    pl.semaphore_wait(barrier, len(OTHERS) + others)

    hops = []
    for k, (dy, dz) in enumerate(OTHERS):
        device = at((y + dy) % 4, (z + dz) % 4)
        copy = remote(masks.at[z, y], masks.at[z, y], mask_send, mask_recv, k, device)
        copy.start()
        hops.append(copy)
    for copy in hops:
        copy.wait_recv()

    hidden_in.wait()
    peer = {"rep": 1 - rep}
    share = hidden.shape[1] // count
    eighth = pl.ds(pl.multiple_of(tp * share, share), share)
    to_peer = remote(hidden.at[:, eighth], hpeer.at[:, eighth], side_send, side_recv, 0, peer)
    to_peer.start()
    ahead = send_hidden(hidden, land_hidden, tail_send, tail_recv)
    first, second, over = route(masks, y, z)
    one_first, one_second, two_first, two_second = offsets(first, second)
    sidx_in.wait()
    index = widen(ring_order(sidx_v[...]))
    table = first_tables(masks, index, first, one_first, one_second, y, z, pool.shape[0])
    row, _ = grid(16, 128)
    one_v[...] = jnp.where(row == 4, jnp.broadcast_to(over, (16, 128)).astype(jnp.int32), table)
    one_in = pltpu.make_async_copy(one_v, one_s, local.at[8])
    one_in.start()
    pool_in.wait()
    one_in.wait()
    over_o[0] = one_s[4, 0]

    def pack(dst, begin, count, src, table, line):
        unroll = 8

        def body(i, _):
            for u in range(unroll):
                p = i * unroll + u
                dst[begin + p] = src[table[line, p]]
            return 0

        lax.fori_loop(0, count // unroll, body, 0)
        for p in range(count // unroll * unroll, count):
            dst[begin + p] = src[table[line, p]]

    stay_one = STAY + 3 * CAP_ONE
    stay_two = STAY + 3 * CAP_TWO
    started = []
    for d in FAR:
        for way, line, device in ((0, (y + d) % 4, at((y + d) % 4, z)), (1, 8 + (z + d) % 4, at(y, (z + d) % 4))):
            begin = (way * 3 + d - 1) * CAP_ONE
            pack(stage_one, begin, CAP_ONE, pool, one_s, line)
            copy = remote(
                stage_one.at[pl.ds(begin, CAP_ONE)],
                mid.at[way, pl.ds(STAY + (d - 1) * CAP_ONE, CAP_ONE)],
                send, recv, way * 3 + d - 1, device,
            )
            copy.start()
            started.append(copy)
    wkv_in.start()
    wq_in.start()
    w_in.start()
    to_peer.wait_recv()
    shared = []
    for k in range(1, count):
        copy = remote(
            hpeer.at[:, eighth], hpeer.at[:, eighth], side_send, side_recv, 1 + k, {"tp": (tp + k) % count}
        )
        copy.start()
        shared.append(copy)
    pack(mid.at[0], 0, STAY, pool, one_s, y)
    pack(mid.at[1], 0, STAY, pool, one_s, 8 + z)

    two_v[...] = second_tables(first, second, one_first, one_second, two_first, two_second, y, z)
    two_in = pltpu.make_async_copy(two_v, two_s, local.at[9])
    two_in.start()
    inv_v[...] = final_table(slots, first, two_first, two_second, y, z)
    inv_in = pltpu.make_async_copy(inv_v, inv_s, local.at[10])
    inv_in.start()

    gain_in.wait()
    for copy in shared:
        copy.wait_recv()
    width = hidden.shape[1]
    step = 1024
    rows = hidden.shape[0]

    def scale_of(ref):
        total = jnp.zeros((rows, 1), jnp.float32)
        for i in range(width // step):
            part = ref[:, i * step : (i + 1) * step].astype(jnp.float32)
            total = total + jnp.sum(part * part, axis=1, keepdims=True)
        return lax.rsqrt(total / width + 1e-05)

    own_scale, peer_scale = scale_of(hidden), scale_of(hpeer)
    for i in range(width // step):
        cut = slice(i * step, (i + 1) * step)
        g = gain[:, cut]
        normed[0:rows, cut] = (hidden[:, cut].astype(jnp.float32) * own_scale * g).astype(jnp.bfloat16)
        normed[rows : 2 * rows, cut] = (hpeer[:, cut].astype(jnp.float32) * peer_scale * g).astype(jnp.bfloat16)

    def product(count, weight):
        def body(i, total):
            cut = pl.ds(pl.multiple_of(i * step, step), step)
            return total + jnp.dot(normed[0:count, cut], weight[cut, :], preferred_element_type=jnp.float32)

        return lax.fori_loop(0, width // step, body, jnp.zeros((count, weight.shape[1]), jnp.float32))

    wkv_in.wait()
    both = product(2 * rows, wkv).astype(jnp.bfloat16)
    kvsend[...] = both[rows : 2 * rows]
    back = remote(kvsend, kvpeer, side_send, side_recv, 1, peer)
    back.start()
    wq_in.wait()
    query = product(rows, wq).astype(jnp.bfloat16).astype(jnp.float32)
    q_o[...] = jnp.zeros_like(q_o)
    for h in range(query.shape[1] // HD):
        q_o[:, h, :] = query[:, h * HD : (h + 1) * HD]
    back.wait_recv()
    mine = jnp.where(holder[0] == rep, jnp.float32(1), jnp.float32(0))
    own = both[0:rows].astype(jnp.float32)
    other = kvpeer[...].astype(jnp.float32)
    kv_o[...] = jnp.where(jnp.full(own.shape, mine) > 0.5, own, other).astype(jnp.bfloat16)

    two_in.wait()
    for copy in started:
        copy.wait_recv()
    relays = []
    for d in FAR:
        for way, line, device in ((0, (z + d) % 4, at(y, (z + d) % 4)), (1, 8 + (y + d) % 4, at((y + d) % 4, z))):
            begin = (way * 3 + d - 1) * CAP_TWO
            pack(stage_two, begin, CAP_TWO, mid.at[way], two_s, line)
            copy = remote(
                stage_two.at[pl.ds(begin, CAP_TWO)],
                fin.at[pl.ds(way * stay_two + STAY + (d - 1) * CAP_TWO, CAP_TWO)],
                send, recv, 6 + way * 3 + d - 1, device,
            )
            copy.start()
            relays.append(copy)
    for way, line in ((0, z), (1, 8 + y)):
        pack(fin, way * stay_two, STAY, mid.at[way], two_s, line)
    inv_in.wait()
    w_in.wait()
    for copy in [to_peer, back, *hops, *shared, *started]:
        copy.wait_send()
    for copy in relays:
        copy.wait_recv()

    per = held.shape[0] // rows
    extra = 2 * stay_two
    for b in range(rows):
        length = lengths[b]
        changed_blocks[b] = renewed(fin[inv_s[0, b * per + length // BLK]], length, kv_o[b : b + 1, :])
    fin[extra : extra + rows] = changed_blocks[...]

    def order(b, _):
        changed = lengths[b] // BLK
        for i in range(per):
            source = jnp.where(changed == i, extra + b, inv_s[0, b * per + i])
            held[b * per + i] = fin[source]
        return 0

    lax.fori_loop(0, rows, order, 0)
    store = pltpu.make_async_copy(held, cache, local.at[11])
    store.start()
    for b in range(rows):
        attention(held, q_o, lengths, att, b)
    attended = side_by_side(att, w.shape[0] // HD)
    summed(attended, w, out, give, kept, paired, land, land_hidden, mate_in, tail_send, tail_recv, ahead)
    for copy in relays:
        copy.wait_send()
    store.wait()


def hand_kernel(source, cache, held, read, written):
    count = read.shape[0]
    per = source.shape[0] // count
    reads, writes = [], []
    for i in range(count):
        part = pl.ds(i * per, per)
        reads.append(pltpu.make_async_copy(source.at[part], held.at[part], read.at[i]))
        writes.append(pltpu.make_async_copy(held.at[part], cache.at[part], written.at[i]))
    for copy in reads:
        copy.start()
    for one, other in zip(reads, writes, strict=True):
        one.wait()
        other.start()
    for copy in writes:
        copy.wait()


def whole_kernel(sidx, pool_h, land, pool, stage, send, recv, local):
    y, z, _ = place()
    pool_in = pltpu.make_async_copy(pool_h, pool, local.at[0])
    pool_in.start()
    pairs = [(dy, dz) for dy in range(4) for dz in range(4) if dy or dz]
    barrier = pltpu.get_barrier_semaphore()
    for dy, dz in pairs:
        pl.semaphore_signal(barrier, inc=1, device_id=at((y + dy) % 4, (z + dz) % 4), device_id_type=MESH)
    pl.semaphore_wait(barrier, len(pairs))
    pool_in.wait()
    me = group(y, z)
    copies = []
    for dy, dz in [(0, 0), *pairs]:
        g = group((y + dy) % 4, (z + dz) % 4)
        k = dy * 4 + dz

        def body(c, _):
            stage[k, c] = pool[sidx[g, c]]
            return 0

        lax.fori_loop(0, stage.shape[1], body, 0)
        if k:
            copy = remote(stage.at[k], land.at[me], send, recv, k - 1, at((y + dy) % 4, (z + dz) % 4))
        else:
            copy = pltpu.make_async_copy(stage.at[0], land.at[me], local.at[1])
        copy.start()
        copies.append(copy)
    for copy in copies:
        copy.wait()


def attention(held, q, lengths, att, b):
    per = held.shape[0] // q.shape[0]
    keys = held[b * per : (b + 1) * per, :, 0:HD].reshape(CTX, HD)
    values = held[b * per : (b + 1) * per, :, HD : 2 * HD].reshape(CTX, HD)
    scores = lax.dot_general(
        q[b].astype(jnp.bfloat16), keys, (((1,), (1,)), ((), ())), preferred_element_type=jnp.float32
    ) * HD ** (-0.5)
    valid = lax.broadcasted_iota(jnp.int32, scores.shape, 1) <= lengths[b]
    expo = jnp.where(valid, jnp.exp(jnp.where(valid, scores, 0.0)), 0.0)
    weights = (expo / jnp.sum(expo, axis=1, keepdims=True)).astype(jnp.bfloat16)
    att[b] = jnp.dot(weights, values, preferred_element_type=jnp.float32)


def side_by_side(att, heads):
    return jnp.concatenate([att[:, h, :] for h in range(heads)], axis=1).astype(jnp.bfloat16)


def renewed(block, length, fresh):
    row, _ = grid(*block.shape)
    fresh = jnp.broadcast_to(fresh.astype(jnp.float32), block.shape)
    return jnp.where(row == length % BLK, fresh, block.astype(jnp.float32)).astype(jnp.bfloat16)


def attend_kernel(inv, lengths, land, q, kv, cache, out, held, att, ready, stored):
    requests = q.shape[0]
    per = held.shape[0] // requests

    def span(b):
        return pl.ds(b * per, per)

    def fetch(b, _):
        for u in range(per):
            j = b * per + u
            pltpu.make_async_copy(land.at[inv[j]], held.at[j], ready.at[b]).start()
        return 0

    lax.fori_loop(0, requests, fetch, 0)
    stores = []
    for b in range(requests):
        pltpu.make_async_copy(land.at[pl.ds(0, per)], held.at[span(b)], ready.at[b]).wait()
        length = lengths[b]
        j = b * per + length // BLK
        held[j] = renewed(held[j], length, kv[b : b + 1, :])
        store = pltpu.make_async_copy(held.at[span(b)], cache.at[span(b)], stored.at[b])
        store.start()
        stores.append(store)
        attention(held, q, lengths, att, b)
    out[...] = side_by_side(att, out.shape[1] // HD)
    for store in stores:
        store.wait()


def summed(attended, w, out, give, own, paired, land, land_hidden, mate_in, send, recv, arriving):
    tp = lax.axis_index("tp")
    section = lax.axis_index("section")
    chips = give.shape[0]
    step = give.shape[2]
    core, chip = tp % 2, tp // 2
    mate = {"tp": chip * 2 + 1 - core}
    after = (section + 1) % lax.axis_size("section")

    def cut(t):
        return pl.ds(pl.multiple_of(t * step, step), step)

    def along(d):
        return ((chip + d) % chips) * 2 + core

    def term(t):
        return jnp.dot(attended, w[:, cut(t)], preferred_element_type=jnp.float32)

    for x in range(chips):
        give[x] = term(x * 2 + 1 - core).astype(jnp.bfloat16)
    swap = remote(give, mate_in, send, recv, 0, mate)
    swap.start()
    for x in range(chips):
        own[x] = term(x * 2 + core)
    swap.wait_recv()
    sums = []
    for d in LONG:
        x = (chip + d) % chips
        paired[d] = (own[x] + mate_in[x].astype(jnp.float32)).astype(jnp.bfloat16)
        copy = remote(paired.at[d], land.at[d], send, recv, 2 + d, {"section": after, "tp": along(d)})
        copy.start()
        sums.append(copy)
    arriving.wait_recv()
    total = land_hidden[...].astype(jnp.float32)
    for copy, d in zip(sums, LONG, strict=True):
        copy.wait_recv()
        total = total + land[d].astype(jnp.float32)
    out[:, cut(tp)] = total.astype(jnp.bfloat16)

    spread = {}
    for d in LONG[:3]:
        copy = remote(out.at[:, cut(tp)], out.at[:, cut(tp)], send, recv, 6 + d, {"tp": along(d)})
        copy.start()
        spread[d] = copy
    passed = [remote(out.at[:, cut(tp)], out.at[:, cut(tp)], send, recv, 10, mate)]
    passed[0].start()
    for d in FAR:
        spread[d].wait_recv()
        t = along(chips - d)
        onward = remote(out.at[:, cut(t)], out.at[:, cut(t)], send, recv, 10 + d, mate)
        onward.start()
        passed.append(onward)
    for copy in passed:
        copy.wait_recv()
    for copy in [swap, arriving, *sums, *spread.values(), *passed]:
        copy.wait_send()


def announce(barrier):
    tp = lax.axis_index("tp")
    section = lax.axis_index("section")
    sections = lax.axis_size("section")
    count = lax.axis_size("tp")
    before = (section + sections - 1) % sections
    for d in range(count // 2):
        pl.semaphore_signal(
            barrier, inc=1, device_id={"section": before, "tp": (tp + 2 * d) % count}, device_id_type=MESH
        )
    for k in range(1, count):
        pl.semaphore_signal(barrier, inc=1, device_id={"tp": (tp + k) % count}, device_id_type=MESH)
    return count // 2 + count - 1


def send_hidden(hidden, land_hidden, send, recv):
    tp = lax.axis_index("tp")
    step = land_hidden.shape[1]
    after = (lax.axis_index("section") + 1) % lax.axis_size("section")
    own = pl.ds(pl.multiple_of(tp * step, step), step)
    ahead = remote(hidden.at[:, own], land_hidden, send, recv, 1, {"section": after})
    ahead.start()
    return ahead


def finish_kernel(attended, hidden, w, out, give, own, paired, land, land_hidden, mate_in, send, recv):
    barrier = pltpu.get_barrier_semaphore()
    pl.semaphore_wait(barrier, announce(barrier))
    ahead = send_hidden(hidden, land_hidden, send, recv)
    summed(attended[...], w, out, give, own, paired, land, land_hidden, mate_in, send, recv, ahead)


def shards(
    hidden, gain, w_query, w_keyval, w_out, old_pool, send_index, recv_slot, holder, lengths
):
    state = hidden[0, 0]
    requests, width = state.shape
    pool_blocks, blk, lanes = old_pool.shape
    groups, cap = send_index.shape[1:]
    blocks = requests * CTX // blk
    heads = w_query.shape[2] // HD
    vmem = pl.BlockSpec(memory_space=pltpu.VMEM)
    smem = pl.BlockSpec(memory_space=pltpu.SMEM)
    hbm = pl.BlockSpec(memory_space=pl.ANY)

    tp = lax.axis_size("tp")
    chips = tp // 2
    chunk = width // tp
    dma = pltpu.SemaphoreType.DMA
    blocks_of = jax.ShapeDtypeStruct((blocks, blk, lanes), jnp.bfloat16)
    rows_of = jax.ShapeDtypeStruct((requests, width), jnp.bfloat16)
    tail = [
        pltpu.VMEM((chips, requests, chunk), jnp.bfloat16),
        pltpu.VMEM((chips, requests, chunk), jnp.float32),
        pltpu.VMEM((chips, requests, chunk), jnp.bfloat16),
        pltpu.VMEM((chips, requests, chunk), jnp.bfloat16),
        pltpu.VMEM((requests, chunk), jnp.bfloat16),
        pltpu.VMEM((chips, requests, chunk), jnp.bfloat16),
    ]

    def params(limit, **more):
        return pltpu.CompilerParams(vmem_limit_bytes=limit * MIB, **more)

    quick_cache, quick_passed, query, keyval, over = pl.pallas_call(
        step_kernel,
        name="step",
        out_shape=(
            blocks_of,
            rows_of,
            jax.ShapeDtypeStruct((requests, 8, HD), jnp.float32),
            jax.ShapeDtypeStruct((requests, lanes), jnp.bfloat16),
            jax.ShapeDtypeStruct((1,), jnp.int32),
        ),
        in_specs=[hbm, hbm, smem, smem, hbm, hbm, hbm, hbm, hbm, hbm],
        out_specs=(hbm, vmem, vmem, vmem, smem),
        scratch_shapes=[
            pltpu.VMEM((groups, cap), jnp.int32),
            pltpu.VMEM((groups, cap), jnp.int32),
            pltpu.VMEM((pool_blocks, blk, lanes), jnp.bfloat16),
            pltpu.VMEM((4, 4, 8, 128), jnp.float32),
            pltpu.VMEM((16, 128), jnp.int32),
            pltpu.VMEM((16, 128), jnp.int32),
            pltpu.VMEM((1, blocks), jnp.int32),
            pltpu.SMEM((16, 128), jnp.int32),
            pltpu.SMEM((16, 128), jnp.int32),
            pltpu.SMEM((1, blocks), jnp.int32),
            pltpu.VMEM((6 * CAP_ONE, blk, lanes), jnp.bfloat16),
            pltpu.VMEM((2, STAY + 3 * CAP_ONE, blk, lanes), jnp.bfloat16),
            pltpu.VMEM((6 * CAP_TWO, blk, lanes), jnp.bfloat16),
            pltpu.VMEM((2 * (STAY + 3 * CAP_TWO) + requests, blk, lanes), jnp.bfloat16),
            pltpu.VMEM((requests, blk, lanes), jnp.bfloat16),
            pltpu.VMEM((blocks, blk, lanes), jnp.bfloat16),
            pltpu.VMEM(w_query.shape[1:], jnp.bfloat16),
            pltpu.VMEM(w_keyval.shape[2:], jnp.bfloat16),
            pltpu.VMEM(w_out.shape[1:], jnp.bfloat16),
            pltpu.VMEM((requests, width), jnp.bfloat16),
            pltpu.VMEM((1, width), jnp.float32),
            pltpu.VMEM((requests, width), jnp.bfloat16),
            pltpu.VMEM((requests, lanes), jnp.bfloat16),
            pltpu.VMEM((requests, lanes), jnp.bfloat16),
            pltpu.VMEM((2 * requests, width), jnp.bfloat16),
            pltpu.VMEM((requests, 8, HD), jnp.float32),
            *tail,
            dma((12,)),
            dma((12,)),
            dma((tp + 1,)),
            dma((tp + 1,)),
            dma((len(OTHERS),)),
            dma((len(OTHERS),)),
            dma((14,)),
            dma((14,)),
            dma((12,)),
        ],
        compiler_params=params(62, collective_id=0, has_side_effects=True),
    )(
        recv_slot[0], send_index[0], holder, lengths[0, 0], state, gain, old_pool, w_query[0], w_keyval[0, 0], w_out[0]
    )

    def quick():
        handed = pl.pallas_call(
            hand_kernel,
            name="hand",
            out_shape=blocks_of,
            in_specs=[hbm],
            out_specs=hbm,
            scratch_shapes=[pltpu.VMEM((blocks, blk, lanes), jnp.bfloat16), dma((4,)), dma((4,))],
            compiler_params=params(60),
        )(quick_cache)
        return handed, quick_passed

    def whole():
        arrived = pl.pallas_call(
            whole_kernel,
            name="whole",
            out_shape=jax.ShapeDtypeStruct((groups, cap, blk, lanes), jnp.bfloat16),
            in_specs=[smem, hbm],
            out_specs=hbm,
            scratch_shapes=[
                pltpu.VMEM((pool_blocks, blk, lanes), jnp.bfloat16),
                pltpu.VMEM((groups, cap, blk, lanes), jnp.bfloat16),
                dma((15,)),
                dma((15,)),
                dma((2,)),
            ],
            compiler_params=params(60, collective_id=2, has_side_effects=True),
        )(send_index[0], old_pool)
        hit = recv_slot[0].reshape(1, -1) == jnp.arange(blocks, dtype=jnp.int32)[:, None]
        inverse = jnp.sum(jnp.where(hit, jnp.arange(groups * cap, dtype=jnp.int32)[None, :], 0), axis=1)
        cache, attended = pl.pallas_call(
            attend_kernel,
            name="attend",
            out_shape=(blocks_of, jax.ShapeDtypeStruct((requests, heads * HD), jnp.bfloat16)),
            in_specs=[smem, smem, hbm, vmem, vmem],
            out_specs=(hbm, vmem),
            scratch_shapes=[
                pltpu.VMEM((blocks, blk, lanes), jnp.bfloat16),
                pltpu.VMEM((requests, 8, HD), jnp.float32),
                dma((requests,)),
                dma((requests,)),
            ],
            compiler_params=params(60),
        )(inverse, lengths[0, 0], arrived.reshape(groups * cap, blk, lanes), query, keyval)
        passed = pl.pallas_call(
            finish_kernel,
            name="finish",
            out_shape=rows_of,
            in_specs=[vmem, vmem, vmem],
            out_specs=vmem,
            scratch_shapes=[*tail, dma((14,)), dma((14,))],
            compiler_params=params(57, collective_id=1, has_side_effects=True),
        )(attended, state, w_out[0])
        return cache, passed

    cache, passed = lax.cond(over[0] > 0, whole, quick)
    return passed[None, None], cache.reshape(1, 1, requests, CTX, lanes)


def solution(mesh):
    in_specs = (
        P("rep", "section", None, None),
        P("section", None),
        P("section", None, "tp"),
        P("rep", "section", None, "tp"),
        P("section", "tp", None),
        P(("rep", "section"), None, "tp"),
        P(("rep", "section"), None, None),
        P(("rep", "section"), None, None),
        P("section"),
        P("rep", "section", None),
    )
    out_specs = (P("rep", "section", None, None), P("rep", "section", None, None, "tp"))
    return jax.shard_map(shards, mesh=mesh, in_specs=in_specs, out_specs=out_specs, check_vma=False)
```

```python
import functools

import jax
import jax.numpy as jnp
from jax import lax
from jax.experimental import pallas as pl
from jax.experimental.pallas import tpu as pltpu
from jax.sharding import PartitionSpec as P

HD = 128
CTX = 512
BLK = 32
MESH = pl.DeviceIdType.MESH
MIB = 2**20
FAR = (1, 3, 2)
LONG = (2, 1, 3, 0)
OTHERS = sorted(
    ((dy, dz) for dy in range(4) for dz in range(4) if dy or dz),
    key=lambda d: -(min(d[0], 4 - d[0]) + min(d[1], 4 - d[1])),
)
CAP_ONE = 41
CAP_TWO = 41
STAY = 128
BALANCE = (0.016, 0.01, 0.006)


def place():
    rep, section = lax.axis_index("rep"), lax.axis_index("section")
    return (section // 4) * 2 + rep, section % 4, lax.axis_index("tp")


def at(y, z):
    return {"rep": y % 2, "section": (y // 2) * 4 + z}


def group(y, z):
    return (y % 2) * 8 + (y // 2) * 4 + z


def remote(src, dst, send, recv, k, device):
    return pltpu.make_async_remote_copy(
        src_ref=src,
        dst_ref=dst,
        send_sem=send.at[k],
        recv_sem=recv.at[k],
        device_id=device,
        device_id_type=MESH,
    )


def dot(a, b):
    return jnp.dot(a.astype(jnp.bfloat16), b.astype(jnp.bfloat16), preferred_element_type=jnp.float32)


def dot_t(a, b):
    return lax.dot_general(
        a.astype(jnp.bfloat16), b.astype(jnp.bfloat16), (((1,), (1,)), ((), ())), preferred_element_type=jnp.float32
    )


def grid(rows, columns):
    return (
        lax.broadcasted_iota(jnp.int32, (rows, columns), 0),
        lax.broadcasted_iota(jnp.int32, (rows, columns), 1),
    )


def ones(condition):
    return jnp.where(condition, 1.0, 0.0).astype(jnp.float32)


def ring_order(table):
    return jnp.concatenate([table[0:4], table[8:12], table[4:8], table[12:16]], axis=0).astype(jnp.float32)


def widen(table):
    k, lane = grid(32, 128)
    return dot(table, ones(k == lane % 32))


def pack_y(table):
    row, lane = grid(16, 128)
    r, k = grid(8, 16)
    return dot(ones(k // 4 == r), jnp.where(lane // 32 == row % 4, table, 0.0))


def pack_z(table):
    row, lane = grid(16, 128)
    r, k = grid(8, 16)
    return dot(ones((k % 4 == r) & (r < 4)), jnp.where(lane // 32 == row // 4, table, 0.0))


def ranks(valid):
    k, lane = grid(128, 128)
    return dot(valid, ones((k < lane) & (k // 32 == lane // 32)))


def route(masks, y, z):
    flat = masks[...].reshape(128, 128)
    k, lane = grid(128, 128)
    per = dot(flat, ones((k // 32 == lane % 4) & (lane < 16)))
    per = jnp.where((lane // 4 == k % 8) & (lane < 16), per, 0.0)
    g, k = grid(16, 128)
    counts = dot(ones(k // 8 == (g % 4) * 4 + g // 4), per)

    g, h = grid(16, 128)
    inside = h < 16
    off_y = ones((g // 4 != h // 4) & inside)
    off_z = ones((g % 4 != h % 4) & inside)
    a, b = grid(16, 16)
    same_y, same_z = ones(a // 4 == b // 4), ones(a % 4 == b % 4)
    a, b = grid(128, 128)
    both = (a < 16) & (b < 16)
    along_y, along_z = ones((a // 4 == b // 4) & both), ones((a % 4 == b % 4) & both)

    def loads(first, second):
        return (
            dot(same_y, first) * off_y,
            dot(same_z, second) * off_z,
            dot(first, along_z) * off_z,
            dot(second, along_y) * off_y,
        )

    share = jnp.full((16, 128), 0.5, jnp.float32)
    for pace in BALANCE:
        a1, b1, a2, b2 = loads(counts * share, counts - counts * share)
        share = jnp.clip(share + pace * (jnp.maximum(b1, b2) - jnp.maximum(a1, a2)), 0.0, 1.0)
    share = jnp.where(g == h, 1.0, share)
    first = jnp.floor(counts * share + 0.5)
    second = counts - first
    a1, b1, a2, b2 = loads(first, second)
    over = jnp.maximum(jnp.maximum(a1, b1) - CAP_ONE, jnp.maximum(a2, b2) - CAP_TWO)
    return first, second, jnp.max(over, keepdims=True)


def offsets(first, second):
    a, b = grid(16, 16)
    one_first = dot(ones((a // 4 == b // 4) & (b % 4 < a % 4)), first)
    one_second = dot(ones((a % 4 == b % 4) & (b // 4 < a // 4)), second)
    a, b = grid(128, 128)
    both = (a < 16) & (b < 16)
    two_first = dot(first, ones((a % 4 == b % 4) & (a // 4 < b // 4) & both))
    two_second = dot(second, ones((a // 4 == b // 4) & (a % 4 < b % 4) & both))
    return one_first, one_second, two_first, two_second


def first_tables(masks, index, first, one_first, one_second, y, z, blocks_held):
    flat = masks[...].reshape(128, 128)
    g, k = grid(16, 128)
    mine = dot(ones(k == ((g % 4) * 4 + g // 4) * 8 + y), flat)
    k, lane = grid(128, 128)
    mine = dot(mine, ones(k == z * 32 + lane % 32))
    g, h = grid(16, 128)

    def column(table):
        picked = jnp.sum(jnp.where(h == y * 4 + z, table, 0.0), axis=1, keepdims=True)
        return jnp.broadcast_to(picked, (16, 128))

    taken = column(first)
    place, lane = grid(128, 128)
    row, _ = grid(8, 128)
    out = []
    for pack, start, is_first in ((pack_y, one_first, True), (pack_z, one_second, False)):
        valid = pack(mine)
        rank = ranks(valid)
        limit = pack(taken)
        begin = pack(column(start))
        blocks = pack(index)
        if is_first:
            keep, at_place = (valid > 0.5) & (rank < limit), begin + rank
        else:
            keep, at_place = (valid > 0.5) & (rank >= limit), begin + rank - limit
        at_place = jnp.where(keep, at_place, -1.0)
        table = jnp.zeros((8, 128), jnp.float32)
        for m in range(4):
            hit = ones(at_place[m : m + 1, :].astype(jnp.int32) == place)
            table = jnp.where(row == m, dot_t(blocks, hit), table)
        out.append(table)
    return jnp.clip(jnp.concatenate(out, axis=0).astype(jnp.int32), 0, blocks_held - 1)


def second_tables(first, second, one_first, one_second, two_first, two_second, y, z):
    r, k = grid(8, 16)
    row, lane = grid(8, 128)
    spot = lane.astype(jnp.float32)
    last = STAY + 3 * CAP_ONE - 1
    out = []
    for count, one, two, rows, me, far in (
        (first, one_first, two_first, ones((k == y * 4 + r) & (r < 4)), y, lambda i: i * 4 + z),
        (second, one_second, two_second, ones((k == r * 4 + z) & (r < 4)), z, lambda i: y * 4 + i),
    ):
        count, one, two = dot(rows, count), dot(rows, one), dot(rows, two)
        table = jnp.zeros((8, 128), jnp.float32)
        for i in range(4):
            pick = lane == far(i)
            n = jnp.sum(jnp.where(pick, count, 0.0), axis=1, keepdims=True)
            begin = jnp.sum(jnp.where(pick, one, 0.0), axis=1, keepdims=True)
            shift = jnp.sum(jnp.where(pick, two, 0.0), axis=1, keepdims=True)
            base = part_of((me - i + 4) % 4, CAP_ONE)
            inside = (spot >= shift) & (spot < shift + n)
            table = jnp.where(inside, begin + spot - shift + jnp.full((8, 128), base).astype(jnp.float32), table)
        out.append(table)
    return jnp.clip(jnp.concatenate(out, axis=0).astype(jnp.int32), 0, last)


def part_of(distance, cap):
    return jnp.where(distance == 0, 0, STAY + (distance - 1) * cap)


def final_table(slots, first, two_first, two_second, y, z):
    valid = ones(slots < 255.5)
    rank = ranks(valid)
    r, k = grid(8, 16)
    row, lane = grid(8, 128)
    a, b = grid(128, 128)
    spread = ones((a % 4 == b // 32) & (a < 16))

    def own(table):
        picked = dot(ones(k == y * 4 + z), table)
        return dot(jnp.where((lane // 4 == row) & (lane < 16), picked, 0.0), spread)

    limit, shift_first, shift_second = own(first), own(two_first), own(two_second)
    total = STAY + 3 * CAP_TWO
    base_first = part_of((z - lane // 32 + 4) % 4, CAP_TWO).astype(jnp.float32)
    base_second = (part_of((y - row + 8) % 4, CAP_TWO) + total).astype(jnp.float32)
    spot = jnp.where(rank < limit, base_first + shift_first + rank, base_second + shift_second + rank - limit)
    spot = jnp.clip(spot, 0.0, float(2 * total - 1))
    high = jnp.floor(spot / 16.0)
    low = spot - high * 16.0
    place, _ = grid(256, 128)
    found = jnp.zeros((8, 256), jnp.float32)
    for m in range(4):
        hit = ones(slots[m : m + 1, :].astype(jnp.int32) == place)
        found = found + dot_t(jnp.where(row == m, high, 0.0), hit) * 16.0 + dot_t(jnp.where(row == m, low, 0.0), hit)
    return jnp.clip(jnp.sum(found, axis=0, keepdims=True).astype(jnp.int32), 0, 2 * total - 1)


def step_kernel(
    recv_h, sidx_h, holder, lengths, hidden_h, gain_h, pool_h, wq_h, wkv_h, w_h,
    cache, out, q_o, kv_o, over_o,
    recv_v, sidx_v, pool, masks, one_v, two_v, inv_v, one_s, two_s, inv_s, stage_one, mid, stage_two, fin, changed_blocks, held,
    wq, wkv, w, hidden, gain, hpeer, kvsend, kvpeer, normed, att, give, kept, paired, land, land_hidden, mate_in,
    send, recv, side_send, side_recv, mask_send, mask_recv, tail_send, tail_recv, local,
):
    y, z, tp = place()
    rep = lax.axis_index("rep")
    count = lax.axis_size("tp")
    copies = [
        pltpu.make_async_copy(src, dst, local.at[i])
        for i, (src, dst) in enumerate(
            ((recv_h, recv_v), (sidx_h, sidx_v), (hidden_h, hidden), (pool_h, pool), (gain_h, gain), (wkv_h, wkv), (wq_h, wq), (w_h, w))
        )
    ]
    recv_in, sidx_in, hidden_in, pool_in, gain_in, wkv_in, wq_in, w_in = copies
    for copy in copies[:5]:
        copy.start()

    barrier = pltpu.get_barrier_semaphore()
    others = announce(barrier)
    for dy, dz in OTHERS:
        device = at((y + dy) % 4, (z + dz) % 4)
        pl.semaphore_signal(barrier, inc=1, device_id=device, device_id_type=MESH)

    recv_in.wait()
    row, _ = grid(8, 128)
    slots = jnp.where(row < 4, pack_y(widen(ring_order(recv_v[...]))), 256.0)
    masks[z, y] = ones(slots < 255.5)
    pl.semaphore_wait(barrier, len(OTHERS) + others)

    hops = []
    for k, (dy, dz) in enumerate(OTHERS):
        device = at((y + dy) % 4, (z + dz) % 4)
        copy = remote(masks.at[z, y], masks.at[z, y], mask_send, mask_recv, k, device)
        copy.start()
        hops.append(copy)
    for copy in hops:
        copy.wait_recv()

    hidden_in.wait()
    peer = {"rep": 1 - rep}
    share = hidden.shape[1] // count
    eighth = pl.ds(pl.multiple_of(tp * share, share), share)
    to_peer = remote(hidden.at[:, eighth], hpeer.at[:, eighth], side_send, side_recv, 0, peer)
    to_peer.start()
    ahead = send_hidden(hidden, land_hidden, tail_send, tail_recv)
    first, second, over = route(masks, y, z)
    one_first, one_second, two_first, two_second = offsets(first, second)
    sidx_in.wait()
    index = widen(ring_order(sidx_v[...]))
    table = first_tables(masks, index, first, one_first, one_second, y, z, pool.shape[0])
    row, _ = grid(16, 128)
    one_v[...] = jnp.where(row == 4, jnp.broadcast_to(over, (16, 128)).astype(jnp.int32), table)
    one_in = pltpu.make_async_copy(one_v, one_s, local.at[8])
    one_in.start()
    pool_in.wait()
    one_in.wait()
    over_o[0] = one_s[4, 0]

    def pack(dst, begin, count, src, table, line):
        unroll = 8

        def body(i, _):
            for u in range(unroll):
                p = i * unroll + u
                dst[begin + p] = src[table[line, p]]
            return 0

        lax.fori_loop(0, count // unroll, body, 0)
        for p in range(count // unroll * unroll, count):
            dst[begin + p] = src[table[line, p]]

    stay_one = STAY + 3 * CAP_ONE
    stay_two = STAY + 3 * CAP_TWO
    started = []
    for d in FAR:
        for way, line, device in ((0, (y + d) % 4, at((y + d) % 4, z)), (1, 8 + (z + d) % 4, at(y, (z + d) % 4))):
            begin = (way * 3 + d - 1) * CAP_ONE
            pack(stage_one, begin, CAP_ONE, pool, one_s, line)
            copy = remote(
                stage_one.at[pl.ds(begin, CAP_ONE)],
                mid.at[way, pl.ds(STAY + (d - 1) * CAP_ONE, CAP_ONE)],
                send, recv, way * 3 + d - 1, device,
            )
            copy.start()
            started.append(copy)
    wkv_in.start()
    wq_in.start()
    w_in.start()
    to_peer.wait_recv()
    shared = []
    for k in range(1, count):
        copy = remote(
            hpeer.at[:, eighth], hpeer.at[:, eighth], side_send, side_recv, 1 + k, {"tp": (tp + k) % count}
        )
        copy.start()
        shared.append(copy)
    pack(mid.at[0], 0, STAY, pool, one_s, y)
    pack(mid.at[1], 0, STAY, pool, one_s, 8 + z)

    two_v[...] = second_tables(first, second, one_first, one_second, two_first, two_second, y, z)
    two_in = pltpu.make_async_copy(two_v, two_s, local.at[9])
    two_in.start()
    inv_v[...] = final_table(slots, first, two_first, two_second, y, z)
    inv_in = pltpu.make_async_copy(inv_v, inv_s, local.at[10])
    inv_in.start()

    gain_in.wait()
    for copy in shared:
        copy.wait_recv()
    width = hidden.shape[1]
    step = 1024
    rows = hidden.shape[0]

    def scale_of(ref):
        total = jnp.zeros((rows, 1), jnp.float32)
        for i in range(width // step):
            part = ref[:, i * step : (i + 1) * step].astype(jnp.float32)
            total = total + jnp.sum(part * part, axis=1, keepdims=True)
        return lax.rsqrt(total / width + 1e-05)

    own_scale, peer_scale = scale_of(hidden), scale_of(hpeer)
    for i in range(width // step):
        cut = slice(i * step, (i + 1) * step)
        g = gain[:, cut]
        normed[0:rows, cut] = (hidden[:, cut].astype(jnp.float32) * own_scale * g).astype(jnp.bfloat16)
        normed[rows : 2 * rows, cut] = (hpeer[:, cut].astype(jnp.float32) * peer_scale * g).astype(jnp.bfloat16)

    def product(count, weight):
        def body(i, total):
            cut = pl.ds(pl.multiple_of(i * step, step), step)
            return total + jnp.dot(normed[0:count, cut], weight[cut, :], preferred_element_type=jnp.float32)

        return lax.fori_loop(0, width // step, body, jnp.zeros((count, weight.shape[1]), jnp.float32))

    wkv_in.wait()
    both = product(2 * rows, wkv).astype(jnp.bfloat16)
    kvsend[...] = both[rows : 2 * rows]
    back = remote(kvsend, kvpeer, side_send, side_recv, 1, peer)
    back.start()
    wq_in.wait()
    query = product(rows, wq).astype(jnp.bfloat16).astype(jnp.float32)
    q_o[...] = jnp.zeros_like(q_o)
    for h in range(query.shape[1] // HD):
        q_o[:, h, :] = query[:, h * HD : (h + 1) * HD]
    back.wait_recv()
    mine = jnp.where(holder[0] == rep, jnp.float32(1), jnp.float32(0))
    own = both[0:rows].astype(jnp.float32)
    other = kvpeer[...].astype(jnp.float32)
    kv_o[...] = jnp.where(jnp.full(own.shape, mine) > 0.5, own, other).astype(jnp.bfloat16)

    two_in.wait()
    for copy in started:
        copy.wait_recv()
    relays = []
    for d in FAR:
        for way, line, device in ((0, (z + d) % 4, at(y, (z + d) % 4)), (1, 8 + (y + d) % 4, at((y + d) % 4, z))):
            begin = (way * 3 + d - 1) * CAP_TWO
            pack(stage_two, begin, CAP_TWO, mid.at[way], two_s, line)
            copy = remote(
                stage_two.at[pl.ds(begin, CAP_TWO)],
                fin.at[pl.ds(way * stay_two + STAY + (d - 1) * CAP_TWO, CAP_TWO)],
                send, recv, 6 + way * 3 + d - 1, device,
            )
            copy.start()
            relays.append(copy)
    for way, line in ((0, z), (1, 8 + y)):
        pack(fin, way * stay_two, STAY, mid.at[way], two_s, line)
    inv_in.wait()
    w_in.wait()
    for copy in [to_peer, back, *hops, *shared, *started]:
        copy.wait_send()
    for copy in relays:
        copy.wait_recv()

    per = held.shape[0] // rows
    extra = 2 * stay_two
    for b in range(rows):
        length = lengths[b]
        changed_blocks[b] = renewed(fin[inv_s[0, b * per + length // BLK]], length, kv_o[b : b + 1, :])
    fin[extra : extra + rows] = changed_blocks[...]

    def order(b, _):
        changed = lengths[b] // BLK
        for i in range(per):
            source = jnp.where(changed == i, extra + b, inv_s[0, b * per + i])
            held[b * per + i] = fin[source]
        return 0

    lax.fori_loop(0, rows, order, 0)
    store = pltpu.make_async_copy(held, cache, local.at[11])
    store.start()
    for b in range(rows):
        attention(held, q_o, lengths, att, b)
    attended = side_by_side(att, w.shape[0] // HD)
    summed(attended, w, out, give, kept, paired, land, land_hidden, mate_in, tail_send, tail_recv, ahead)
    for copy in relays:
        copy.wait_send()
    store.wait()


def hand_kernel(source, passed, cache, out, held, read, written):
    count = read.shape[0]
    per = source.shape[0] // count
    reads, writes = [], []
    for i in range(count):
        part = pl.ds(i * per, per)
        reads.append(pltpu.make_async_copy(source.at[part], held.at[part], read.at[i]))
        writes.append(pltpu.make_async_copy(held.at[part], cache.at[part], written.at[i]))
    writes.append(pltpu.make_async_copy(passed, out, written.at[count]))
    for copy in reads:
        copy.start()
    writes[count].start()
    for i in range(count):
        reads[i].wait()
        writes[i].start()
    for copy in writes:
        copy.wait()


def whole_kernel(sidx, pool_h, land, pool, stage, send, recv, local):
    y, z, _ = place()
    pool_in = pltpu.make_async_copy(pool_h, pool, local.at[0])
    pool_in.start()
    pairs = [(dy, dz) for dy in range(4) for dz in range(4) if dy or dz]
    barrier = pltpu.get_barrier_semaphore()
    for dy, dz in pairs:
        pl.semaphore_signal(barrier, inc=1, device_id=at((y + dy) % 4, (z + dz) % 4), device_id_type=MESH)
    pl.semaphore_wait(barrier, len(pairs))
    pool_in.wait()
    me = group(y, z)
    copies = []
    for dy, dz in [(0, 0), *pairs]:
        g = group((y + dy) % 4, (z + dz) % 4)
        k = dy * 4 + dz

        def body(c, _):
            stage[k, c] = pool[sidx[g, c]]
            return 0

        lax.fori_loop(0, stage.shape[1], body, 0)
        if k:
            copy = remote(stage.at[k], land.at[me], send, recv, k - 1, at((y + dy) % 4, (z + dz) % 4))
        else:
            copy = pltpu.make_async_copy(stage.at[0], land.at[me], local.at[1])
        copy.start()
        copies.append(copy)
    for copy in copies:
        copy.wait()


def attention(held, q, lengths, att, b):
    per = held.shape[0] // q.shape[0]
    keys = held[b * per : (b + 1) * per, :, 0:HD].reshape(CTX, HD)
    values = held[b * per : (b + 1) * per, :, HD : 2 * HD].reshape(CTX, HD)
    scores = lax.dot_general(
        q[b].astype(jnp.bfloat16), keys, (((1,), (1,)), ((), ())), preferred_element_type=jnp.float32
    ) * HD ** (-0.5)
    valid = lax.broadcasted_iota(jnp.int32, scores.shape, 1) <= lengths[b]
    expo = jnp.where(valid, jnp.exp(jnp.where(valid, scores, 0.0)), 0.0)
    weights = (expo / jnp.sum(expo, axis=1, keepdims=True)).astype(jnp.bfloat16)
    att[b] = jnp.dot(weights, values, preferred_element_type=jnp.float32)


def side_by_side(att, heads):
    return jnp.concatenate([att[:, h, :] for h in range(heads)], axis=1).astype(jnp.bfloat16)


def renewed(block, length, fresh):
    row, _ = grid(*block.shape)
    fresh = jnp.broadcast_to(fresh.astype(jnp.float32), block.shape)
    return jnp.where(row == length % BLK, fresh, block.astype(jnp.float32)).astype(jnp.bfloat16)


def attend_kernel(inv, lengths, land, q, kv, cache, out, held, att, ready, stored):
    requests = q.shape[0]
    per = held.shape[0] // requests

    def span(b):
        return pl.ds(b * per, per)

    def fetch(b, _):
        for u in range(per):
            j = b * per + u
            pltpu.make_async_copy(land.at[inv[j]], held.at[j], ready.at[b]).start()
        return 0

    lax.fori_loop(0, requests, fetch, 0)
    stores = []
    for b in range(requests):
        pltpu.make_async_copy(land.at[pl.ds(0, per)], held.at[span(b)], ready.at[b]).wait()
        length = lengths[b]
        j = b * per + length // BLK
        held[j] = renewed(held[j], length, kv[b : b + 1, :])
        store = pltpu.make_async_copy(held.at[span(b)], cache.at[span(b)], stored.at[b])
        store.start()
        stores.append(store)
        attention(held, q, lengths, att, b)
    out[...] = side_by_side(att, out.shape[1] // HD)
    for store in stores:
        store.wait()


def summed(attended, w, out, give, own, paired, land, land_hidden, mate_in, send, recv, arriving):
    tp = lax.axis_index("tp")
    section = lax.axis_index("section")
    chips = give.shape[0]
    step = give.shape[2]
    core, chip = tp % 2, tp // 2
    mate = {"tp": chip * 2 + 1 - core}
    after = (section + 1) % lax.axis_size("section")

    def cut(t):
        return pl.ds(pl.multiple_of(t * step, step), step)

    def along(d):
        return ((chip + d) % chips) * 2 + core

    def term(t):
        return jnp.dot(attended, w[:, cut(t)], preferred_element_type=jnp.float32)

    for x in range(chips):
        give[x] = term(x * 2 + 1 - core).astype(jnp.bfloat16)
    swap = remote(give, mate_in, send, recv, 0, mate)
    swap.start()
    for x in range(chips):
        own[x] = term(x * 2 + core)
    swap.wait_recv()
    sums = []
    for d in LONG:
        x = (chip + d) % chips
        paired[d] = (own[x] + mate_in[x].astype(jnp.float32)).astype(jnp.bfloat16)
        copy = remote(paired.at[d], land.at[d], send, recv, 2 + d, {"section": after, "tp": along(d)})
        copy.start()
        sums.append(copy)
    arriving.wait_recv()
    total = land_hidden[...].astype(jnp.float32)
    for copy, d in zip(sums, LONG, strict=True):
        copy.wait_recv()
        total = total + land[d].astype(jnp.float32)
    out[:, cut(tp)] = total.astype(jnp.bfloat16)

    spread = {}
    for d in LONG[:3]:
        copy = remote(out.at[:, cut(tp)], out.at[:, cut(tp)], send, recv, 6 + d, {"tp": along(d)})
        copy.start()
        spread[d] = copy
    passed = [remote(out.at[:, cut(tp)], out.at[:, cut(tp)], send, recv, 10, mate)]
    passed[0].start()
    for d in FAR:
        spread[d].wait_recv()
        t = along(chips - d)
        onward = remote(out.at[:, cut(t)], out.at[:, cut(t)], send, recv, 10 + d, mate)
        onward.start()
        passed.append(onward)
    for copy in passed:
        copy.wait_recv()
    for copy in [swap, arriving, *sums, *spread.values(), *passed]:
        copy.wait_send()


def announce(barrier):
    tp = lax.axis_index("tp")
    section = lax.axis_index("section")
    sections = lax.axis_size("section")
    count = lax.axis_size("tp")
    before = (section + sections - 1) % sections
    for d in range(count // 2):
        pl.semaphore_signal(
            barrier, inc=1, device_id={"section": before, "tp": (tp + 2 * d) % count}, device_id_type=MESH
        )
    for k in range(1, count):
        pl.semaphore_signal(barrier, inc=1, device_id={"tp": (tp + k) % count}, device_id_type=MESH)
    return count // 2 + count - 1


def send_hidden(hidden, land_hidden, send, recv):
    tp = lax.axis_index("tp")
    step = land_hidden.shape[1]
    after = (lax.axis_index("section") + 1) % lax.axis_size("section")
    own = pl.ds(pl.multiple_of(tp * step, step), step)
    ahead = remote(hidden.at[:, own], land_hidden, send, recv, 1, {"section": after})
    ahead.start()
    return ahead


def finish_kernel(attended, hidden, w, out, give, own, paired, land, land_hidden, mate_in, send, recv):
    barrier = pltpu.get_barrier_semaphore()
    pl.semaphore_wait(barrier, announce(barrier))
    ahead = send_hidden(hidden, land_hidden, send, recv)
    summed(attended[...], w, out, give, own, paired, land, land_hidden, mate_in, send, recv, ahead)


def shards(
    hidden, gain, w_query, w_keyval, w_out, old_pool, send_index, recv_slot, holder, lengths
):
    state = hidden[0, 0]
    requests, width = state.shape
    pool_blocks, blk, lanes = old_pool.shape
    groups, cap = send_index.shape[1:]
    blocks = requests * CTX // blk
    heads = w_query.shape[2] // HD
    vmem = pl.BlockSpec(memory_space=pltpu.VMEM)
    smem = pl.BlockSpec(memory_space=pltpu.SMEM)
    hbm = pl.BlockSpec(memory_space=pl.ANY)

    tp = lax.axis_size("tp")
    chips = tp // 2
    chunk = width // tp
    dma = pltpu.SemaphoreType.DMA
    blocks_of = jax.ShapeDtypeStruct((blocks, blk, lanes), jnp.bfloat16)
    rows_of = jax.ShapeDtypeStruct((requests, width), jnp.bfloat16)
    tail = [
        pltpu.VMEM((chips, requests, chunk), jnp.bfloat16),
        pltpu.VMEM((chips, requests, chunk), jnp.float32),
        pltpu.VMEM((chips, requests, chunk), jnp.bfloat16),
        pltpu.VMEM((chips, requests, chunk), jnp.bfloat16),
        pltpu.VMEM((requests, chunk), jnp.bfloat16),
        pltpu.VMEM((chips, requests, chunk), jnp.bfloat16),
    ]

    def params(limit, **more):
        return pltpu.CompilerParams(vmem_limit_bytes=limit * MIB, **more)

    quick_cache, quick_passed, query, keyval, over = pl.pallas_call(
        step_kernel,
        name="step",
        out_shape=(
            blocks_of,
            rows_of,
            jax.ShapeDtypeStruct((requests, 8, HD), jnp.float32),
            jax.ShapeDtypeStruct((requests, lanes), jnp.bfloat16),
            jax.ShapeDtypeStruct((1,), jnp.int32),
        ),
        in_specs=[hbm, hbm, smem, smem, hbm, hbm, hbm, hbm, hbm, hbm],
        out_specs=(hbm, vmem, vmem, vmem, smem),
        scratch_shapes=[
            pltpu.VMEM((groups, cap), jnp.int32),
            pltpu.VMEM((groups, cap), jnp.int32),
            pltpu.VMEM((pool_blocks, blk, lanes), jnp.bfloat16),
            pltpu.VMEM((4, 4, 8, 128), jnp.float32),
            pltpu.VMEM((16, 128), jnp.int32),
            pltpu.VMEM((16, 128), jnp.int32),
            pltpu.VMEM((1, blocks), jnp.int32),
            pltpu.SMEM((16, 128), jnp.int32),
            pltpu.SMEM((16, 128), jnp.int32),
            pltpu.SMEM((1, blocks), jnp.int32),
            pltpu.VMEM((6 * CAP_ONE, blk, lanes), jnp.bfloat16),
            pltpu.VMEM((2, STAY + 3 * CAP_ONE, blk, lanes), jnp.bfloat16),
            pltpu.VMEM((6 * CAP_TWO, blk, lanes), jnp.bfloat16),
            pltpu.VMEM((2 * (STAY + 3 * CAP_TWO) + requests, blk, lanes), jnp.bfloat16),
            pltpu.VMEM((requests, blk, lanes), jnp.bfloat16),
            pltpu.VMEM((blocks, blk, lanes), jnp.bfloat16),
            pltpu.VMEM(w_query.shape[1:], jnp.bfloat16),
            pltpu.VMEM(w_keyval.shape[2:], jnp.bfloat16),
            pltpu.VMEM(w_out.shape[1:], jnp.bfloat16),
            pltpu.VMEM((requests, width), jnp.bfloat16),
            pltpu.VMEM((1, width), jnp.float32),
            pltpu.VMEM((requests, width), jnp.bfloat16),
            pltpu.VMEM((requests, lanes), jnp.bfloat16),
            pltpu.VMEM((requests, lanes), jnp.bfloat16),
            pltpu.VMEM((2 * requests, width), jnp.bfloat16),
            pltpu.VMEM((requests, 8, HD), jnp.float32),
            *tail,
            dma((12,)),
            dma((12,)),
            dma((tp + 1,)),
            dma((tp + 1,)),
            dma((len(OTHERS),)),
            dma((len(OTHERS),)),
            dma((14,)),
            dma((14,)),
            dma((12,)),
        ],
        compiler_params=params(62, collective_id=0, has_side_effects=True),
    )(
        recv_slot[0], send_index[0], holder, lengths[0, 0], state, gain, old_pool, w_query[0], w_keyval[0, 0], w_out[0]
    )

    def hand(cache, passed):
        return pl.pallas_call(
            hand_kernel,
            name="hand",
            out_shape=(blocks_of, rows_of),
            in_specs=[hbm, vmem],
            out_specs=(hbm, hbm),
            scratch_shapes=[pltpu.VMEM((blocks, blk, lanes), jnp.bfloat16), dma((4,)), dma((5,))],
            compiler_params=params(60),
        )(cache, passed)

    def quick():
        return hand(quick_cache, quick_passed)

    def whole():
        arrived = pl.pallas_call(
            whole_kernel,
            name="whole",
            out_shape=jax.ShapeDtypeStruct((groups, cap, blk, lanes), jnp.bfloat16),
            in_specs=[smem, hbm],
            out_specs=hbm,
            scratch_shapes=[
                pltpu.VMEM((pool_blocks, blk, lanes), jnp.bfloat16),
                pltpu.VMEM((groups, cap, blk, lanes), jnp.bfloat16),
                dma((15,)),
                dma((15,)),
                dma((2,)),
            ],
            compiler_params=params(60, collective_id=2, has_side_effects=True),
        )(send_index[0], old_pool)
        hit = recv_slot[0].reshape(1, -1) == jnp.arange(blocks, dtype=jnp.int32)[:, None]
        inverse = jnp.sum(jnp.where(hit, jnp.arange(groups * cap, dtype=jnp.int32)[None, :], 0), axis=1)
        cache, attended = pl.pallas_call(
            attend_kernel,
            name="attend",
            out_shape=(blocks_of, jax.ShapeDtypeStruct((requests, heads * HD), jnp.bfloat16)),
            in_specs=[smem, smem, hbm, vmem, vmem],
            out_specs=(hbm, vmem),
            scratch_shapes=[
                pltpu.VMEM((blocks, blk, lanes), jnp.bfloat16),
                pltpu.VMEM((requests, 8, HD), jnp.float32),
                dma((requests,)),
                dma((requests,)),
            ],
            compiler_params=params(60),
        )(inverse, lengths[0, 0], arrived.reshape(groups * cap, blk, lanes), query, keyval)
        passed = pl.pallas_call(
            finish_kernel,
            name="finish",
            out_shape=rows_of,
            in_specs=[vmem, vmem, vmem],
            out_specs=vmem,
            scratch_shapes=[*tail, dma((14,)), dma((14,))],
            compiler_params=params(57, collective_id=1, has_side_effects=True),
        )(attended, state, w_out[0])
        return hand(cache, passed)

    cache, passed = lax.cond(over[0] > 0, whole, quick)
    return passed[None, None], cache.reshape(1, 1, requests, CTX, lanes)


def solution(mesh):
    in_specs = (
        P("rep", "section", None, None),
        P("section", None),
        P("section", None, "tp"),
        P("rep", "section", None, "tp"),
        P("section", "tp", None),
        P(("rep", "section"), None, "tp"),
        P(("rep", "section"), None, None),
        P(("rep", "section"), None, None),
        P("section"),
        P("rep", "section", None),
    )
    out_specs = (P("rep", "section", None, None), P("rep", "section", None, None, "tp"))
    return jax.shard_map(shards, mesh=mesh, in_specs=in_specs, out_specs=out_specs, check_vma=False)
```
